512 devices in a mesh: dp: 16 (over x, z_hi, core), fsdp: 4 (over y), tensor: 8 (over z_lo).
Axes of the slice: x: 4, y: 4, z: 16 (z_hi: 2, z_lo: 8; z = z_hi * 8 + z_lo), core: 2. Of those that a mesh axis runs over, the one named last changes fastest.
Arguments:
- tokens: bfloat16 [65536, 576], P(('dp', 'fsdp', 'tensor')), may hold values from -6 to 6
- gate_weight: bfloat16 [576, 1536], P('fsdp', 'tensor'), may hold values from -0.25 to 0.25
- up_weight: bfloat16 [576, 1536], P('fsdp', 'tensor'), may hold values from -0.25 to 0.25
- down_weight: bfloat16 [1536, 576], P('tensor', 'fsdp'), may hold values from -0.15625 to 0.15625
- cotangent: bfloat16 [65536, 576], P(('dp', 'fsdp', 'tensor')), may hold values from -0.119628906 to 0.119628906
Outputs:
- mixed: bfloat16 [65536, 576], P(('dp', 'fsdp', 'tensor'))
- grad_tokens: bfloat16 [65536, 576], P(('dp', 'fsdp', 'tensor'))
- grad_gate_weight: bfloat16 [576, 1536], P('fsdp', 'tensor')
- grad_up_weight: bfloat16 [576, 1536], P('fsdp', 'tensor')
- grad_down_weight: bfloat16 [1536, 576], P('tensor', 'fsdp')
The draws below stay inside these ranges and needn't reach their ends.
All inputs are finite; a program needn't handle non-finite values.
Results may differ from the reference program's by a relative error of at most 0.025.
Values may be sent and summed in bfloat16 or wider, within the bound.
A program may use at most 64 MiB of HBM per device.

```python
import math
import jax
import jax.numpy as jnp
from jax import lax

D = 576
FF = 1536
TOKENS = 65536
N_TENSOR = 8


def block_levels(stream_key, shape, split, smallest, high):
    gain = 1.0
    for dim, blocks in split:
        heights = jax.random.uniform(jax.random.fold_in(jax.random.fold_in(stream_key, 6), dim), (blocks,), jnp.float32, smallest / len(split), high / len(split))
        gain = gain * jnp.repeat(jnp.exp(heights), shape[dim] // blocks).reshape((-1,) + (1,) * (len(shape) - 1 - dim))
    return gain


def centred(key, extent, scale, most, cuts=(), kind=jnp.bfloat16):
    loudness = block_levels(key, extent, cuts, -0.22, 0.18) if cuts else 1.0
    array = jax.random.normal(key, extent, jnp.float32) * scale * loudness
    return jnp.minimum(jnp.maximum(array, -most), most).astype(kind)


def setup_inputs(seed: int = 0) -> dict:
    seeds = jax.random.split(jax.random.key(seed), 6)
    return {
        "tokens": centred(seeds[0], (TOKENS, D), 1.0, 6.0, ((0, 512),)),
        "gate_weight": centred(seeds[1], (D, FF), D ** -0.5, 0.25, ((0, 4), (1, 8))),
        "up_weight": centred(seeds[2], (D, FF), D ** -0.5, 0.25, ((0, 4), (1, 8))),
        "down_weight": centred(seeds[3], (FF, D), FF ** -0.5, 0.15625, ((0, 8), (1, 4))),
        "cotangent": centred(seeds[4], (TOKENS, D), 0.02, 0.119628906, ((0, 512),)),
    }


def activate(gate_sum, up_sum):
    sig = jax.nn.sigmoid(gate_sum)
    swished = gate_sum * sig
    slopes = up_sum * sig * (1.0 + gate_sum * (1.0 - sig))
    hidden = (swished * up_sum).astype(jnp.bfloat16)
    return hidden, swished, slopes


def inner_rows(left, right):
    return lax.dot_general(left, right, (((0,), (0,)), ((), ())), preferred_element_type=jnp.float32)


def inner_cols(left, right):
    return lax.dot_general(left, right, (((1,), (1,)), ((), ())), preferred_element_type=jnp.float32)


def group_sum(pairs, blocks):
    total = None
    for left, right in pairs:
        rows = left.shape[0]
        width = left.shape[1] // blocks
        left_blocks = left.reshape(rows, blocks, width).astype(jnp.float32)
        right_blocks = right.reshape(blocks, width, right.shape[1]).astype(jnp.float32)
        term = jnp.einsum("rtk,tkd->trd", left_blocks, right_blocks)
        total = term if total is None else total + term
    rounded = lax.optimization_barrier(total.astype(jnp.bfloat16))
    return jnp.sum(rounded.astype(jnp.float32), axis=0)


def reference(tokens, gate_weight, up_weight, down_weight, cotangent):
    block = math.gcd(TOKENS, 4096)
    count = TOKENS // block
    gate_back = gate_weight.T
    up_back = up_weight.T

    def step(carry, index):
        acc_gate, acc_up, acc_down = carry
        first = (index * block).astype(jnp.int32)
        rows = lax.dynamic_slice_in_dim(tokens, first, block, 0)
        cot_rows = lax.dynamic_slice_in_dim(cotangent, first, block, 0)
        gate_sum = jnp.dot(rows, gate_weight, preferred_element_type=jnp.float32)
        up_sum = jnp.dot(rows, up_weight, preferred_element_type=jnp.float32)
        hidden, swished, slopes = activate(gate_sum, up_sum)
        mixed = group_sum(((hidden, down_weight),), N_TENSOR).astype(jnp.bfloat16)
        grad_hidden = inner_cols(cot_rows, down_weight)
        grad_gate = (grad_hidden * slopes).astype(jnp.bfloat16)
        grad_up = (grad_hidden * swished).astype(jnp.bfloat16)
        grad_rows = group_sum(((grad_gate, gate_back), (grad_up, up_back)), N_TENSOR).astype(jnp.bfloat16)
        acc_gate = acc_gate + inner_rows(rows, grad_gate)
        acc_up = acc_up + inner_rows(rows, grad_up)
        acc_down = acc_down + inner_rows(hidden, cot_rows)
        return (acc_gate, acc_up, acc_down), (mixed, grad_rows)

    start = (jnp.zeros((D, FF), jnp.float32), jnp.zeros((D, FF), jnp.float32), jnp.zeros((FF, D), jnp.float32))
    sums, outs = lax.scan(step, start, jnp.arange(count, dtype=jnp.int32))
    mixed = outs[0].reshape(TOKENS, D)
    grad_tokens = outs[1].reshape(TOKENS, D)
    return mixed, grad_tokens, sums[0].astype(jnp.bfloat16), sums[1].astype(jnp.bfloat16), sums[2].astype(jnp.bfloat16)
```

```python
import jax
import jax.numpy as jnp
from jax import lax
from jax.experimental import pallas as pl
from jax.experimental.pallas import tpu as pltpu
from jax.sharding import PartitionSpec as P

MESH = pl.DeviceIdType.MESH
F32 = jnp.float32
BF16 = jnp.bfloat16

D = 576
ROWS = 128
DY = 144
HID = 192
CHUNKS = 3
CROWS = DY // CHUNKS
TILES = 48
PIECE = TILES // 8


def tn(left, right):
    return lax.dot_general(left, right, (((0,), (0,)), ((), ())), preferred_element_type=F32)


def nt(left, right):
    return lax.dot_general(left, right, (((1,), (1,)), ((), ())), preferred_element_type=F32)


def nn(left, right):
    return jnp.dot(left, right, preferred_element_type=F32)


def kernel(
    tok_ref, gate_ref, up_ref, down_ref, cot_ref,
    mixed_ref, gtok_ref, ggate_ref, gup_ref, gdown_ref,
    xs, wpack, wall, ggu, hid, sib_out, own, sib_in, xsend, xrecv,
    ysend, yrecv, zsend, zrecv, tiles, rsrecv, zhsend, zhrecv, fin,
    tok_s, tok_r, fwd_s, fwd_r, wz_s, wz_r, wy_s, wy_r,
    sib_s, sib_r, tr_s, tr_r, gy_s, gy_r, gz_s, gz_r, rs_s, rs_r, zh_s, zh_r, ag_s, ag_r,
):
    dp = lax.axis_index("dp")
    y = lax.axis_index("fsdp")
    zl = lax.axis_index("tensor")
    x, zh, c = dp // 4, (dp // 2) % 2, dp % 2
    z = zh * 8 + zl
    sib_c = 1 - c

    def dev(xx, yy, zz, cc):
        zz = (zz + 16) % 16
        return ((xx % 4) * 4 + (zz // 8) * 2 + cc, yy % 4, zz % 8)

    def group(dx, dc):
        return dev(x + dx, y, z, c if dc == 0 else sib_c)

    block = (zl + x) % 4 + 4 * c
    k_from = jnp.where((block - zl + 8) % 8 == x, 0, 1)
    k_to = (c + zl // 4) % 2
    local = jnp.logical_and(x == 0, k_to == 0)
    remote = jnp.logical_not(local)
    z_from = dev(x, y, z + x - 4 * k_from, (c + k_from) % 2)
    z_to = dev(x, y, z - x + 4 * k_to, zl // 4)
    zh_dev = dev(x, y, z + 8, c)

    def rcopy(src, dst, ssem, rsem, to):
        return pltpu.make_async_remote_copy(
            src_ref=src, dst_ref=dst, send_sem=ssem, recv_sem=rsem, device_id=to, device_id_type=MESH
        )

    barrier = pltpu.get_barrier_semaphore()

    def greet(to):
        pl.semaphore_signal(barrier, inc=1, device_id=to, device_id_type=MESH)

    for dx in range(4):
        for dc in range(2):
            if dx or dc:
                greet(group(dx, dc))
    for d in (1, 2, 3):
        greet(dev(x, y + d, z, c))
    greet(zh_dev)

    @pl.when(remote)
    def _():
        greet(z_from)
        greet(z_to)

    wpack[:, 0:HID] = gate_ref[...]
    wpack[:, HID : 2 * HID] = up_ref[...]
    eye = (
        lax.broadcasted_iota(jnp.int32, (DY, DY), 0) == lax.broadcasted_iota(jnp.int32, (DY, DY), 1)
    ).astype(BF16)
    wpack[:, 2 * HID : 3 * HID] = nt(eye, down_ref[...]).astype(BF16)
    xs[0, 0] = tok_ref[...].T
    xs[1, 0] = cot_ref[...].T

    @pl.when(remote)
    def _():
        pl.semaphore_wait(barrier, 13)

    @pl.when(local)
    def _():
        pl.semaphore_wait(barrier, 11)

    my_rows = pl.multiple_of(y * DY, 16)

    def chunk(ref, base, i):
        return ref.at[pl.ds(pl.multiple_of(base + i * CROWS, 16), CROWS)]

    wz = [
        rcopy(wpack.at[pl.ds(i * CROWS, CROWS)], chunk(wall, my_rows, i), wz_s.at[i], wz_r.at[i], z_to)
        for i in range(CHUNKS)
    ]

    @pl.when(remote)
    def _():
        for cp in wz:
            cp.start()

    tok = {}
    for a in (0, 1):
        for dx in (2, 1, 3):
            tok[a, dx] = rcopy(
                xs.at[a, 0], xs.at[a, 2 * (4 - dx)], tok_s.at[a, dx], tok_r.at[a, 4 - dx], group(dx, 0)
            )
            tok[a, dx].start()
    fwd = {}
    for a in (0, 1):
        fwd[a, 0] = rcopy(xs.at[a, 0], xs.at[a, 1], fwd_s.at[a, 0], fwd_r.at[a, 0], group(0, 1))
        fwd[a, 0].start()

    @pl.when(local)
    def _():
        wall[pl.ds(my_rows, DY), :] = wpack[...]

    wy = {}
    for i in range(CHUNKS):

        @pl.when(remote)
        def _(i=i):
            wz[i].wait_recv()

        for d in (2, 1, 3):
            wy[i, d] = rcopy(
                chunk(wall, my_rows, i), chunk(wall, my_rows, i), wy_s.at[i, d], wy_r.at[i, 4 - d],
                dev(x, y + d, z, c),
            )
            wy[i, d].start()

    def arrived(ref, sem):
        return rcopy(ref, ref, sem, sem, group(0, 1))

    for a in (0, 1):
        for dx in (1, 3, 2):
            arrived(xs.at[a, 2 * dx], tok_r.at[a, dx]).wait_recv()
            fwd[a, dx] = rcopy(
                xs.at[a, 2 * dx], xs.at[a, 2 * dx + 1], fwd_s.at[a, dx], fwd_r.at[a, dx], group(0, 1)
            )
            fwd[a, dx].start()

    for i in range(CHUNKS):
        for d in (1, 3, 2):
            src_rows = pl.multiple_of(((y + d) % 4) * DY, 16)
            arrived(chunk(wall, src_rows, i), wy_r.at[i, d]).wait_recv()

    for dx in (0, 1, 3, 2):
        cols = pl.ds(dx * 256, 256)
        for a in (0, 1):
            fwd[a, dx].wait_recv()
        tokens = jnp.concatenate([xs[0, 2 * dx], xs[0, 2 * dx + 1]], axis=1)
        cots = jnp.concatenate([xs[1, 2 * dx], xs[1, 2 * dx + 1]], axis=1)
        sums = tn(wall[:, 0 : 2 * HID], tokens)
        grad_hidden = tn(wall[:, 2 * HID : 3 * HID], cots)
        gate_sum, up_sum = sums[0:HID], sums[HID : 2 * HID]
        sig = jax.nn.sigmoid(gate_sum)
        swished = gate_sum * sig
        slopes = up_sum * sig * (1.0 + gate_sum * (1.0 - sig))
        hid[:, cols] = (swished * up_sum).astype(BF16)
        ggu[0:HID, cols] = (grad_hidden * slopes).astype(BF16)
        ggu[HID : 2 * HID, cols] = (grad_hidden * swished).astype(BF16)

    gy = {}
    for d in (2, 1, 3, 0):
        rows = pl.ds(pl.multiple_of(((y + d) % 4) * DY, 16), DY)
        tokens = jnp.concatenate([xs[0, s, rows, :] for s in range(8)], axis=1)
        cots = jnp.concatenate([xs[1, s, rows, :] for s in range(8)], axis=1)
        ysend[d, :, 0 : 2 * HID] = nt(tokens, ggu[...]).astype(BF16)
        ysend[d, :, 2 * HID : 3 * HID] = nt(cots, hid[...]).astype(BF16)
        if d:
            gy[d] = rcopy(ysend.at[d], yrecv.at[4 - d], gy_s.at[d], gy_r.at[4 - d], dev(x, y + d, z, c))
            gy[d].start()

    sib = {}
    for dx in (2, 1, 3, 0):
        cols = pl.ds(dx * 256, 256)
        for a in (0, 1):
            part = nn(wall[:, 2 * HID : 3 * HID], hid[:, cols]) if a == 0 else nn(wall[:, 0 : 2 * HID], ggu[:, cols])
            own[a, dx] = part[:, 0:ROWS]
            sib_out[a, dx] = part[:, ROWS : 2 * ROWS].astype(BF16)
            sib[a, dx] = rcopy(
                sib_out.at[a, dx], sib_in.at[a, dx], sib_s.at[a, dx], sib_r.at[a, dx], group(0, 1)
            )
            sib[a, dx].start()
    tr = {}
    for dx in (2, 1, 3):
        for a in (0, 1):
            sib[a, dx].wait_recv()
            xsend[a, dx] = (own[a, dx] + sib_in[a, dx].astype(F32)).astype(BF16)
            tr[a, dx] = rcopy(
                xsend.at[a, dx], xrecv.at[a, 4 - dx], tr_s.at[a, dx], tr_r.at[a, 4 - dx], group(dx, 0)
            )
            tr[a, dx].start()

    for d in (1, 3, 2):
        arrived(yrecv.at[d], gy_r.at[d]).wait_recv()
    zsend[...] = (
        ysend[0].astype(F32) + yrecv[1].astype(F32) + yrecv[2].astype(F32) + yrecv[3].astype(F32)
    ).astype(BF16)
    gz = rcopy(zsend, zrecv, gz_s, gz_r, z_from)

    @pl.when(remote)
    def _():
        gz.start()

    @pl.when(local)
    def _():
        zrecv[...] = zsend[...]

    for a, out in ((0, mixed_ref), (1, gtok_ref)):
        sib[a, 0].wait_recv()
        total = own[a, 0] + sib_in[a, 0].astype(F32)
        for dx in (1, 3, 2):
            arrived(xrecv.at[a, dx], tr_r.at[a, dx]).wait_recv()
            total = total + xrecv[a, dx].astype(F32)
        out[...] = total.T.astype(BF16)

    @pl.when(remote)
    def _():
        gz.wait_recv()

    for r in range(9):
        for q in range(5):
            width = 128 if q < 4 else 64
            tiles[5 * r + q, :, 0:width] = zrecv[16 * r : 16 * r + 16, 128 * q : 128 * q + width]
            if width < 128:
                tiles[5 * r + q, :, width:128] = jnp.zeros((16, 128 - width), BF16)
    for t in range(45, TILES):
        tiles[t] = jnp.zeros((16, 128), BF16)
    me = x * 2 + c
    rs = {}
    for dx in (2, 1, 3, 0):
        for dc in (1, 0):
            if dx or dc:
                rank = ((x + dx) % 4) * 2 + (c if dc == 0 else sib_c)
                slot = ((4 - dx) % 4) * 2 + dc
                rs[dx, dc] = rcopy(
                    tiles.at[pl.ds(rank * PIECE, PIECE)], rsrecv.at[slot], rs_s.at[dx * 2 + dc], rs_r.at[slot],
                    group(dx, dc),
                )
                rs[dx, dc].start()
    total = tiles[pl.ds(me * PIECE, PIECE)].astype(F32)
    for slot in range(1, 8):
        arrived(rsrecv.at[slot], rs_r.at[slot]).wait_recv()
        total = total + rsrecv[slot].astype(F32)
    zhsend[...] = total.astype(BF16)
    zhc = rcopy(zhsend, zhrecv, zh_s, zh_r, zh_dev)
    zhc.start()
    zhc.wait()
    mine = pl.ds(me * PIECE, PIECE)
    fin[mine] = (zhsend[...].astype(F32) + zhrecv[...].astype(F32)).astype(BF16)
    ag = {}
    for dx in (2, 1, 3, 0):
        for dc in (1, 0):
            if dx or dc:
                slot = ((4 - dx) % 4) * 2 + dc
                ag[dx, dc] = rcopy(
                    fin.at[mine], fin.at[mine], ag_s.at[dx * 2 + dc], ag_r.at[slot], group(dx, dc)
                )
                ag[dx, dc].start()
    for dx in range(4):
        for dc in range(2):
            if dx or dc:
                rank = ((x + dx) % 4) * 2 + (c if dc == 0 else sib_c)
                arrived(fin.at[pl.ds(rank * PIECE, PIECE)], ag_r.at[dx * 2 + dc]).wait_recv()

    whole = jnp.concatenate(
        [jnp.concatenate([fin[5 * r + q] for q in range(5)], axis=1) for r in range(9)], axis=0
    )
    ggate_ref[...] = whole[:, 0:HID]
    gup_ref[...] = whole[:, HID : 2 * HID]
    gdown_ref[...] = tn(whole[:, 2 * HID : 3 * HID], eye).astype(BF16)

    @pl.when(remote)
    def _():
        for cp in wz:
            cp.wait_send()
        gz.wait_send()

    for cps in (tok, fwd, wy, gy, sib, tr, rs, ag):
        for cp in cps.values():
            cp.wait_send()


def per_device(tokens, gate_weight, up_weight, down_weight, cotangent):
    dma = pltpu.SemaphoreType.DMA
    vm = pltpu.VMEM
    outs = (
        jax.ShapeDtypeStruct((ROWS, D), BF16),
        jax.ShapeDtypeStruct((ROWS, D), BF16),
        jax.ShapeDtypeStruct((DY, HID), BF16),
        jax.ShapeDtypeStruct((DY, HID), BF16),
        jax.ShapeDtypeStruct((HID, DY), BF16),
    )
    spec = pl.BlockSpec(memory_space=vm)
    return pl.pallas_call(
        kernel,
        out_shape=outs,
        in_specs=[spec] * 5,
        out_specs=[spec] * 5,
        scratch_shapes=[
            vm((2, 8, D, ROWS), BF16),
            vm((DY, 3 * HID), BF16),
            vm((D, 3 * HID), BF16),
            vm((2 * HID, 8 * ROWS), BF16),
            vm((HID, 8 * ROWS), BF16),
            vm((2, 4, D, ROWS), BF16),
            vm((2, 4, D, ROWS), F32),
            vm((2, 4, D, ROWS), BF16),
            vm((2, 4, D, ROWS), BF16),
            vm((2, 4, D, ROWS), BF16),
            vm((4, DY, 3 * HID), BF16),
            vm((4, DY, 3 * HID), BF16),
            vm((DY, 3 * HID), BF16),
            vm((DY, 3 * HID), BF16),
            vm((TILES, 16, 128), BF16),
            vm((8, PIECE, 16, 128), BF16),
            vm((PIECE, 16, 128), BF16),
            vm((PIECE, 16, 128), BF16),
            vm((TILES, 16, 128), BF16),
            dma((2, 4)), dma((2, 4)),
            dma((2, 4)), dma((2, 4)),
            dma((CHUNKS,)), dma((CHUNKS,)),
            dma((CHUNKS, 4)), dma((CHUNKS, 4)),
            dma((2, 4)), dma((2, 4)),
            dma((2, 4)), dma((2, 4)),
            dma((4,)), dma((4,)),
            dma, dma,
            dma((8,)), dma((8,)),
            dma, dma,
            dma((8,)), dma((8,)),
        ],
        compiler_params=pltpu.CompilerParams(
            collective_id=0, has_side_effects=True, vmem_limit_bytes=48 << 20
        ),
        name="swiglu",
    )(tokens, gate_weight, up_weight, down_weight, cotangent)


def solution(mesh):
    return jax.shard_map(
        per_device,
        mesh=mesh,
        in_specs=(
            P(("dp", "fsdp", "tensor"), None),
            P("fsdp", "tensor"),
            P("fsdp", "tensor"),
            P("tensor", "fsdp"),
            P(("dp", "fsdp", "tensor"), None),
        ),
        out_specs=(
            P(("dp", "fsdp", "tensor"), None),
            P(("dp", "fsdp", "tensor"), None),
            P("fsdp", "tensor"),
            P("fsdp", "tensor"),
            P("tensor", "fsdp"),
        ),
        check_vma=False,
    )
```

```python
import jax
import jax.numpy as jnp
from jax import lax
from jax.experimental import pallas as pl
from jax.experimental.pallas import tpu as pltpu
from jax.sharding import PartitionSpec as P

MESH = pl.DeviceIdType.MESH
F32 = jnp.float32
BF16 = jnp.bfloat16

D = 576
ROWS = 128
DY = 144
HID = 192
TILES = 41
CUTS = (0, 14, 27, 41)
WIDE = 11
HALF = 6


def tn(left, right):
    return lax.dot_general(left, right, (((0,), (0,)), ((), ())), preferred_element_type=F32)


def nt(left, right):
    return lax.dot_general(left, right, (((1,), (1,)), ((), ())), preferred_element_type=F32)


def nn(left, right):
    return jnp.dot(left, right, preferred_element_type=F32)


def store_gate_up(ref, value):
    for r in range(9):
        for q in range(3):
            ref[3 * r + q] = value[16 * r : 16 * r + 16, 128 * q : 128 * q + 128]


def store_down(ref, value):
    for r in range(9):
        ref[27 + r] = value[16 * r : 16 * r + 16, 0:128]
    for i in range(4):
        ref[36 + i] = jnp.concatenate(
            [value[32 * i : 32 * i + 16, 128:192], value[32 * i + 16 : 32 * i + 32, 128:192]], axis=1
        )
    ref[40] = jnp.concatenate([value[128:144, 128:192], jnp.zeros((16, 64), value.dtype)], axis=1)


def load_gate_up(tile):
    return jnp.concatenate(
        [jnp.concatenate([tile(3 * r + q) for q in range(3)], axis=1) for r in range(9)], axis=0
    )


def load_down(tile):
    rows = []
    for r in range(9):
        last = tile(36 + r // 2)
        rows.append(jnp.concatenate([tile(27 + r), last[:, 0:64] if r % 2 == 0 else last[:, 64:128]], axis=1))
    return jnp.concatenate(rows, axis=0)


def kernel(
    tok_ref, gate_ref, up_ref, down_ref, cot_ref,
    mixed_ref, gtok_ref, ggate_ref, gup_ref, gdown_ref,
    xs, win, wmine, wrows, wall, swi, slo, ggu, hid, sib_out, own, sib_in, xsend, xrecv,
    ysend, xyr, zs, zr, zhsend, zhrecv, fin,
    in_s, tok_s, tok_r, fwd_s, fwd_r, wz_s, wz_r, wy_s, wy_r,
    sib_s, sib_r, tr_s, tr_r, xy_s, xy_r, gz_s, gz_r, zh_s, zh_r, ag_s, ag_r,
):
    dp = lax.axis_index("dp")
    y = lax.axis_index("fsdp")
    zl = lax.axis_index("tensor")
    x, zh, c = dp // 4, (dp // 2) % 2, dp % 2
    z = zh * 8 + zl
    sib_c = 1 - c
    home = zl // 4

    def dev(xx, yy, zz, cc):
        zz = (zz + 16) % 16
        return (((xx + 4) % 4) * 4 + (zz // 8) * 2 + cc, (yy + 4) % 4, zz % 8)

    def group(dx, dc):
        return dev(x + dx, y, z, c if dc == 0 else sib_c)

    block = (zl + x) % 4 + 4 * c
    k_from = jnp.where((block - zl + 8) % 8 == x, 0, 1)
    k_to = (c + home) % 2
    local = jnp.logical_and(x == 0, k_to == 0)
    remote = jnp.logical_not(local)
    z_to = dev(x, y, z - x + 4 * k_to, home)
    zh_dev = dev(x, y, z + 8, c)

    shift = [jnp.where(((zl + r) % 4 + 4 * c - zl + 8) % 8 == r, r, r - 4) for r in range(4)]

    def rcopy(src, dst, ssem, rsem, to):
        return pltpu.make_async_remote_copy(
            src_ref=src, dst_ref=dst, send_sem=ssem, recv_sem=rsem, device_id=to, device_id_type=MESH
        )

    inputs = [
        pltpu.make_async_copy(tok_ref, xs.at[0, 0], in_s.at[0]),
        pltpu.make_async_copy(cot_ref, xs.at[1, 0], in_s.at[1]),
        pltpu.make_async_copy(gate_ref, win.at[0], in_s.at[2]),
        pltpu.make_async_copy(up_ref, win.at[1], in_s.at[3]),
        pltpu.make_async_copy(down_ref, win.at[2], in_s.at[4]),
    ]
    for cp in inputs:
        cp.start()

    barrier = pltpu.get_barrier_semaphore()

    def greet(to):
        pl.semaphore_signal(barrier, inc=1, device_id=to, device_id_type=MESH)

    greet(zh_dev)
    for s in (-4, 3, -3, 2, -2, 1, -1):
        greet(dev(x, y, z - s, home))
    for r in (3, 2, 1):
        for h in range(2):
            greet(dev(x, y, z + shift[r], h))

    @pl.when(c != home)
    def _():
        for h in range(2):
            greet(dev(x, y, z - 4, h))

    for dx in (2, 1, 3, 0):
        for d in (2, 1, 3, 0):
            if dx or d:
                greet(dev(x + dx, y + d, z, c))
        greet(group(dx, 1))

    for cp in inputs:
        cp.wait()
    store_gate_up(wmine, jnp.concatenate([win[0], win[1]], axis=1))
    store_down(wmine, win[2])

    @pl.when(c != home)
    def _():
        pl.semaphore_wait(barrier, 35)

    @pl.when(c == home)
    def _():
        pl.semaphore_wait(barrier, 33)

    def cut(ref, i):
        return ref.at[pl.ds(CUTS[i], CUTS[i + 1] - CUTS[i])]

    wz = [
        rcopy(cut(wmine, i), cut(wrows.at[0], i), wz_s.at[i], wz_r.at[i], z_to) for i in range(len(CUTS) - 1)
    ]

    @pl.when(remote)
    def _():
        for cp in wz:
            cp.start()

    tok = {}
    fwd = {}
    for a in (0, 1):
        for dx in (2, 1, 3):
            tok[a, dx] = rcopy(
                xs.at[a, 0], xs.at[a, 2 * (4 - dx)], tok_s.at[a, dx], tok_r.at[a, 4 - dx], group(dx, 0)
            )
            tok[a, dx].start()
    for a in (0, 1):
        fwd[a, 0] = rcopy(xs.at[a, 0], xs.at[a, 1], fwd_s.at[a, 0], fwd_r.at[a, 0], group(0, 1))
        fwd[a, 0].start()

    @pl.when(local)
    def _():
        wrows[0] = wmine[...]

    wy = {}
    for i in range(len(CUTS) - 1):

        @pl.when(remote)
        def _(i=i):
            wz[i].wait_recv()

        for d in (2, 1, 3):
            wy[i, d] = rcopy(
                cut(wrows.at[0], i), cut(wrows.at[4 - d], i), wy_s.at[i, d], wy_r.at[i, 4 - d],
                dev(x, y + d, z, c),
            )
            wy[i, d].start()

    def arrived(ref, sem):
        return rcopy(ref, ref, sem, sem, group(0, 1))

    def pass_on(a):
        for dx in (1, 3, 2):
            arrived(xs.at[a, 2 * dx], tok_r.at[a, dx]).wait_recv()
            fwd[a, dx] = rcopy(
                xs.at[a, 2 * dx], xs.at[a, 2 * dx + 1], fwd_s.at[a, dx], fwd_r.at[a, dx], group(0, 1)
            )
            fwd[a, dx].start()

    def pair(a, dx):
        return jnp.concatenate([xs[a, 2 * dx], xs[a, 2 * dx + 1]], axis=1)

    pass_on(0)
    for i in range(2):
        for d in (1, 3, 2):
            arrived(cut(wrows.at[d], i), wy_r.at[i, d]).wait_recv()
    for d in range(4):
        rows = pl.ds(pl.multiple_of(((y + d) % 4) * DY, 16), DY)
        wall[rows, 0 : 2 * HID] = load_gate_up(lambda t: wrows[d, t])
    for dx in (0, 1, 3, 2):
        cols = pl.ds(dx * 256, 256)
        fwd[0, dx].wait_recv()
        sums = tn(wall[:, 0 : 2 * HID], pair(0, dx))
        gate_sum, up_sum = sums[0:HID], sums[HID : 2 * HID]
        sig = jax.nn.sigmoid(gate_sum)
        swished = gate_sum * sig
        swi[:, cols] = swished
        slo[:, cols] = up_sum * sig * (1.0 + gate_sum * (1.0 - sig))
        hid[:, cols] = (swished * up_sum).astype(BF16)
    pass_on(1)
    for d in (1, 3, 2):
        arrived(cut(wrows.at[d], 2), wy_r.at[2, d]).wait_recv()
    for d in range(4):
        rows = pl.ds(pl.multiple_of(((y + d) % 4) * DY, 16), DY)
        wall[rows, 2 * HID : 3 * HID] = load_down(lambda t: wrows[d, t])
    for dx in (0, 1, 3, 2):
        cols = pl.ds(dx * 256, 256)
        fwd[1, dx].wait_recv()
        grad_hidden = tn(wall[:, 2 * HID : 3 * HID], pair(1, dx))
        ggu[0:HID, cols] = (grad_hidden * slo[:, cols]).astype(BF16)
        ggu[HID : 2 * HID, cols] = (grad_hidden * swi[:, cols]).astype(BF16)

    xy = {}
    for d in (2, 1, 3, 0):
        rows = pl.ds(pl.multiple_of(((y + d) % 4) * DY, 16), DY)
        tokens = jnp.concatenate([xs[0, s, rows, :] for s in range(8)], axis=1)
        cots = jnp.concatenate([xs[1, s, rows, :] for s in range(8)], axis=1)
        store_gate_up(ysend.at[d], nt(tokens, ggu[...]).astype(BF16))
        store_down(ysend.at[d], nt(cots, hid[...]).astype(BF16))
        for dx in (2, 1, 3, 0):
            piece = ysend.at[d, pl.ds(((x + dx) % 4) * 10, WIDE)]
            if d or dx:
                there = ((4 - dx) % 4, (4 - d) % 4)
                xy[dx, d] = rcopy(
                    piece, xyr.at[there[0], there[1]], xy_s.at[dx, d], xy_r.at[there[0], there[1]],
                    dev(x + dx, y + d, z, c),
                )
                xy[dx, d].start()
            else:
                xyr[0, 0] = piece[...]

    sib = {}
    for dx in (2, 1, 3, 0):
        cols = pl.ds(dx * 256, 256)
        for a in (0, 1):
            part = nn(wall[:, 2 * HID : 3 * HID], hid[:, cols]) if a == 0 else nn(wall[:, 0 : 2 * HID], ggu[:, cols])
            own[a, dx] = part[:, 0:ROWS]
            sib_out[a, dx] = part[:, ROWS : 2 * ROWS].astype(BF16)
            sib[a, dx] = rcopy(
                sib_out.at[a, dx], sib_in.at[a, dx], sib_s.at[a, dx], sib_r.at[a, dx], group(0, 1)
            )
            sib[a, dx].start()
    tr = {}
    for dx in (2, 1, 3):
        for a in (0, 1):
            sib[a, dx].wait_recv()
            xsend[a, dx] = (own[a, dx] + sib_in[a, dx].astype(F32)).astype(BF16)
            tr[a, dx] = rcopy(
                xsend.at[a, dx], xrecv.at[a, 4 - dx], tr_s.at[a, dx], tr_r.at[a, 4 - dx], group(dx, 0)
            )

    for dx in (0, 1, 3, 2):
        for d in (0, 1, 3, 2):
            if dx or d:
                arrived(xyr.at[dx, d], xy_r.at[dx, d]).wait_recv()
    gz = {}
    keep = c == home
    for r in (3, 2, 1, 0):
        there = (r - x + 4) % 4
        total = xyr[there, 0].astype(F32)
        for d in (1, 2, 3):
            total = total + xyr[there, d].astype(F32)
        zs[r] = total.astype(BF16)
        slot = shift[r] + 4
        for h in range(2):
            gz[r, h] = rcopy(
                zs.at[r, pl.ds(5 * h, HALF)], zr.at[slot], gz_s.at[r, h], gz_r.at[slot], dev(x, y, z + shift[r], h)
            )
            if r:
                gz[r, h].start()
            else:
                stays = jnp.logical_and(keep, c == h)

                @pl.when(jnp.logical_not(stays))
                def _(h=h):
                    gz[0, h].start()

                @pl.when(stays)
                def _(h=h):
                    zr[4] = zs[0, pl.ds(5 * h, HALF)]

    for dx in (2, 1, 3):
        for a in (0, 1):
            tr[a, dx].start()

    total = None
    for s in (5, 3, 6, 2, 7, 1, 0):
        arrived(zr.at[s], gz_r.at[s]).wait_recv()

    @pl.when(jnp.logical_not(keep))
    def _():
        arrived(zr.at[4], gz_r.at[4]).wait_recv()

    total = zr[0].astype(F32)
    for s in range(1, 8):
        total = total + zr[s].astype(F32)
    zhsend[...] = total.astype(BF16)
    zhc = rcopy(zhsend, zhrecv, zh_s, zh_r, zh_dev)
    zhc.start()

    for a, out in ((0, mixed_ref), (1, gtok_ref)):
        sib[a, 0].wait_recv()
        total = own[a, 0] + sib_in[a, 0].astype(F32)
        for dx in (1, 3, 2):
            arrived(xrecv.at[a, dx], tr_r.at[a, dx]).wait_recv()
            total = total + xrecv[a, dx].astype(F32)
        out[...] = total.astype(BF16)

    zhc.wait()
    me = x * 2 + c
    fin[me] = (zhsend[...].astype(F32) + zhrecv[...].astype(F32)).astype(BF16)
    ag = {}
    for dx in (2, 1, 3, 0):
        for dc in (1, 0):
            if dx or dc:
                slot = ((4 - dx) % 4) * 2 + dc
                ag[dx, dc] = rcopy(fin.at[me], fin.at[me], ag_s.at[dx * 2 + dc], ag_r.at[slot], group(dx, dc))
                ag[dx, dc].start()
    for dx in range(4):
        for dc in range(2):
            if dx or dc:
                rank = ((x + dx) % 4) * 2 + (c if dc == 0 else sib_c)
                arrived(fin.at[rank], ag_r.at[dx * 2 + dc]).wait_recv()

    def summed(t):
        over = min(t // 10, 3)
        half = min((t - 10 * over) // 5, 1)
        return fin[2 * over + half, t - 10 * over - 5 * half]

    whole = load_gate_up(summed)
    ggate_ref[...] = whole[:, 0:HID]
    gup_ref[...] = whole[:, HID : 2 * HID]
    gdown_ref[...] = load_down(summed)

    @pl.when(remote)
    def _():
        for cp in wz:
            cp.wait_send()

    for key, cp in gz.items():
        if key[0]:
            cp.wait_send()
        else:

            @pl.when(jnp.logical_not(jnp.logical_and(keep, c == key[1])))
            def _(cp=cp):
                cp.wait_send()

    for cps in (tok, fwd, wy, xy, sib, tr, ag):
        for cp in cps.values():
            cp.wait_send()


def place(*refs):
    for i, o in zip(refs[:5], refs[5:]):
        o[...] = i[...]


def per_device(tokens, gate_weight, up_weight, down_weight, cotangent):
    dma = pltpu.SemaphoreType.DMA
    vm = pltpu.VMEM
    outs = (
        jax.ShapeDtypeStruct((D, ROWS), BF16),
        jax.ShapeDtypeStruct((D, ROWS), BF16),
        jax.ShapeDtypeStruct((DY, HID), BF16),
        jax.ShapeDtypeStruct((DY, HID), BF16),
        jax.ShapeDtypeStruct((DY, HID), BF16),
    )
    pieces = len(CUTS) - 1
    results = pl.pallas_call(
        kernel,
        out_shape=outs,
        in_specs=[pl.BlockSpec(memory_space=pl.ANY)] * 5,
        out_specs=[pl.BlockSpec(memory_space=vm)] * 5,
        scratch_shapes=[
            vm((2, 8, D, ROWS), BF16),
            vm((3, DY, HID), BF16),
            vm((TILES, 16, 128), BF16),
            vm((4, TILES, 16, 128), BF16),
            vm((D, 3 * HID), BF16),
            vm((HID, 8 * ROWS), F32),
            vm((HID, 8 * ROWS), F32),
            vm((2 * HID, 8 * ROWS), BF16),
            vm((HID, 8 * ROWS), BF16),
            vm((2, 4, D, ROWS), BF16),
            vm((2, 4, D, ROWS), F32),
            vm((2, 4, D, ROWS), BF16),
            vm((2, 4, D, ROWS), BF16),
            vm((2, 4, D, ROWS), BF16),
            vm((4, TILES, 16, 128), BF16),
            vm((4, 4, WIDE, 16, 128), BF16),
            vm((4, WIDE, 16, 128), BF16),
            vm((8, HALF, 16, 128), BF16),
            vm((HALF, 16, 128), BF16),
            vm((HALF, 16, 128), BF16),
            vm((8, HALF, 16, 128), BF16),
            dma((5,)),
            dma((2, 4)), dma((2, 4)),
            dma((2, 4)), dma((2, 4)),
            dma((pieces,)), dma((pieces,)),
            dma((pieces, 4)), dma((pieces, 4)),
            dma((2, 4)), dma((2, 4)),
            dma((2, 4)), dma((2, 4)),
            dma((4, 4)), dma((4, 4)),
            dma((4, 2)), dma((8,)),
            dma, dma,
            dma((8,)), dma((8,)),
        ],
        compiler_params=pltpu.CompilerParams(
            collective_id=0, has_side_effects=True, vmem_limit_bytes=60 << 20
        ),
        name="swiglu",
    )(tokens.T, gate_weight, up_weight, down_weight.T, cotangent.T)
    mixed, gtok, ggate, gup, gdown = pl.pallas_call(
        place,
        out_shape=outs,
        in_specs=[pl.BlockSpec(memory_space=vm)] * 5,
        out_specs=[pl.BlockSpec(memory_space=vm)] * 5,
        name="place",
    )(*results)
    return mixed.T, gtok.T, ggate, gup, gdown.T


def solution(mesh):
    return jax.shard_map(
        per_device,
        mesh=mesh,
        in_specs=(
            P(("dp", "fsdp", "tensor"), None),
            P("fsdp", "tensor"),
            P("fsdp", "tensor"),
            P("tensor", "fsdp"),
            P(("dp", "fsdp", "tensor"), None),
        ),
        out_specs=(
            P(("dp", "fsdp", "tensor"), None),
            P(("dp", "fsdp", "tensor"), None),
            P("fsdp", "tensor"),
            P("fsdp", "tensor"),
            P("tensor", "fsdp"),
        ),
        check_vma=False,
    )
```

```python
import jax
import jax.numpy as jnp
from jax import lax
from jax.experimental import pallas as pl
from jax.experimental.pallas import tpu as pltpu
from jax.sharding import PartitionSpec as P

MESH = pl.DeviceIdType.MESH
F32 = jnp.float32
BF16 = jnp.bfloat16

D = 576
ROWS = 128
DY = 144
HID = 192
TILES = 41
CUTS = (0, 14, 27, 41)
GU_WIDE, DN_WIDE = 7, 4
HALF = 6


def gate_up_start(x):
    return 7 * x - x // 3


def down_start(x):
    return 4 * x - 2 * (x // 3)


def tn(left, right):
    return lax.dot_general(left, right, (((0,), (0,)), ((), ())), preferred_element_type=F32)


def nt(left, right):
    return lax.dot_general(left, right, (((1,), (1,)), ((), ())), preferred_element_type=F32)


def nn(left, right):
    return jnp.dot(left, right, preferred_element_type=F32)


def store_gate_up(ref, value):
    for r in range(9):
        for q in range(3):
            ref[3 * r + q] = value[16 * r : 16 * r + 16, 128 * q : 128 * q + 128]


def store_down(ref, value):
    for r in range(9):
        ref[27 + r] = value[16 * r : 16 * r + 16, 0:128]
    for i in range(4):
        ref[36 + i] = jnp.concatenate(
            [value[32 * i : 32 * i + 16, 128:192], value[32 * i + 16 : 32 * i + 32, 128:192]], axis=1
        )
    ref[40] = jnp.concatenate([value[128:144, 128:192], jnp.zeros((16, 64), value.dtype)], axis=1)


def load_gate_up(tile):
    return jnp.concatenate(
        [jnp.concatenate([tile(3 * r + q) for q in range(3)], axis=1) for r in range(9)], axis=0
    )


def load_down(tile):
    rows = []
    for r in range(9):
        last = tile(36 + r // 2)
        rows.append(jnp.concatenate([tile(27 + r), last[:, 0:64] if r % 2 == 0 else last[:, 64:128]], axis=1))
    return jnp.concatenate(rows, axis=0)


def kernel(
    tok_ref, gate_ref, up_ref, down_ref, cot_ref,
    mixed_ref, gtok_ref, ggate_ref, gup_ref, gdown_ref,
    xs, win, wmine, wrows, wall, swi, slo, ggu, hid, sib_out, own, sib_in, xsend, xrecv, xopp,
    ysend, xyr, zs, zr, zhsend, zhrecv, fin,
    in_s, tok_s, tok_r, fwd_s, fwd_r, wz_s, wz_r, wy_s, wy_r, opp_s, opp_r,
    sib_s, sib_r, tro_s, tro_r, tr_s, tr_r, xy_s, xy_r, gz_s, gz_r, zh_s, zh_r, ag_s, ag_r, far_sem,
):
    dp = lax.axis_index("dp")
    y = lax.axis_index("fsdp")
    zl = lax.axis_index("tensor")
    x, zh, c = dp // 4, (dp // 2) % 2, dp % 2
    z = zh * 8 + zl
    sib_c = 1 - c
    home = zl // 4

    def dev(xx, yy, zz, cc):
        zz = (zz + 16) % 16
        return (((xx + 4) % 4) * 4 + (zz // 8) * 2 + cc, (yy + 4) % 4, zz % 8)

    def group(dx, dc):
        return dev(x + dx, y, z, c if dc == 0 else sib_c)

    block = (zl + x) % 4 + 4 * c
    k_from = jnp.where((block - zl + 8) % 8 == x, 0, 1)
    k_to = (c + home) % 2
    local = jnp.logical_and(x == 0, k_to == 0)
    remote = jnp.logical_not(local)
    z_to = dev(x, y, z - x + 4 * k_to, home)
    zh_dev = dev(x, y, z + 8, c)

    shift = [jnp.where(((zl + r) % 4 + 4 * c - zl + 8) % 8 == r, r, r - 4) for r in range(4)]

    def rcopy(src, dst, ssem, rsem, to):
        return pltpu.make_async_remote_copy(
            src_ref=src, dst_ref=dst, send_sem=ssem, recv_sem=rsem, device_id=to, device_id_type=MESH
        )

    inputs = [
        pltpu.make_async_copy(tok_ref, xs.at[0, 0], in_s.at[0]),
        pltpu.make_async_copy(cot_ref, xs.at[1, 0], in_s.at[1]),
        pltpu.make_async_copy(gate_ref, win.at[0], in_s.at[2]),
        pltpu.make_async_copy(up_ref, win.at[1], in_s.at[3]),
        pltpu.make_async_copy(down_ref, win.at[2], in_s.at[4]),
    ]
    for cp in inputs:
        cp.start()

    barrier = pltpu.get_barrier_semaphore()

    def greet(to):
        pl.semaphore_signal(barrier, inc=1, device_id=to, device_id_type=MESH)

    for s in (4, -4):
        greet(dev(x, y, z + s, c))
    for s in (-4, 3, -3, 2, -2, 1, -1):
        greet(dev(x, y, z - s, home))
    for r in (3, 2, 1):
        for h in range(2):
            greet(dev(x, y, z + shift[r], h))

    @pl.when(c != home)
    def _():
        for h in range(2):
            greet(dev(x, y, z - 4, h))

    for dx in (2, 1, 3, 0):
        for d in (2, 1, 3, 0):
            if dx or d:
                greet(dev(x + dx, y + d, z, c))
        greet(group(dx, 1))

    for cp in inputs:
        cp.wait()
    store_gate_up(wmine, jnp.concatenate([win[0], win[1]], axis=1))
    store_down(wmine, win[2])

    @pl.when(c != home)
    def _():
        pl.semaphore_wait(barrier, 36)

    @pl.when(c == home)
    def _():
        pl.semaphore_wait(barrier, 34)

    pl.semaphore_signal(far_sem, inc=1, device_id=dev(x, y, z - 4, c), device_id_type=MESH)

    def cut(ref, i):
        return ref.at[pl.ds(CUTS[i], CUTS[i + 1] - CUTS[i])]

    wz = [
        rcopy(cut(wmine, i), cut(wrows.at[0], i), wz_s.at[i], wz_r.at[i], z_to) for i in range(len(CUTS) - 1)
    ]

    @pl.when(remote)
    def _():
        for cp in wz:
            cp.start()

    tok = {}
    opp = {}
    fwd = {}
    halves = {1: pl.ds(0, D // 2), 3: pl.ds(D // 2, D // 2)}
    for a in (0, 1):
        for dx in (1, 3):
            tok[a, dx] = rcopy(
                xs.at[a, 0], xs.at[a, 2 * (4 - dx)], tok_s.at[a, dx], tok_r.at[a, 4 - dx], group(dx, 0)
            )
            tok[a, dx].start()
    for a in (0, 1):
        fwd[a, 0] = rcopy(xs.at[a, 0], xs.at[a, 1], fwd_s.at[a, 0], fwd_r.at[a, 0], group(0, 1))
        fwd[a, 0].start()

    @pl.when(local)
    def _():
        wrows[0] = wmine[...]

    def arrived(ref, sem):
        return rcopy(ref, ref, sem, sem, group(0, 1))

    def pass_on(a):
        for dx in (1, 3):
            arrived(xs.at[a, 2 * dx], tok_r.at[a, dx]).wait_recv()
            opp[a, dx] = rcopy(
                xs.at[a, 2 * dx, halves[dx]], xs.at[a, 4, halves[dx]], opp_s.at[a, dx], opp_r.at[a, dx],
                group(4 - dx, 0),
            )
            opp[a, dx].start()
            fwd[a, dx] = rcopy(
                xs.at[a, 2 * dx], xs.at[a, 2 * dx + 1], fwd_s.at[a, dx], fwd_r.at[a, dx], group(0, 1)
            )
            fwd[a, dx].start()

    def pass_on_opposite(a):
        for dx in (1, 3):
            arrived(xs.at[a, 4, halves[dx]], opp_r.at[a, dx]).wait_recv()
            fwd[a, dx + 3] = rcopy(
                xs.at[a, 4, halves[dx]], xs.at[a, 5, halves[dx]], fwd_s.at[a, dx + 3], fwd_r.at[a, dx + 3], group(0, 1)
            )
            fwd[a, dx + 3].start()

    def wait_pair(a, dx):
        for k in (dx,) if dx != 2 else (4, 6):
            fwd[a, k].wait_recv()

    wy = {}

    for i in range(len(CUTS) - 1):

        @pl.when(remote)
        def _(i=i):
            wz[i].wait_recv()

        for d in (2, 1, 3):
            wy[i, d] = rcopy(
                cut(wrows.at[0], i), cut(wrows.at[4 - d], i), wy_s.at[i, d], wy_r.at[i, 4 - d],
                dev(x, y + d, z, c),
            )
            wy[i, d].start()
        if i == 0:
            pass_on(0)

    def pair(a, dx):
        return jnp.concatenate([xs[a, 2 * dx], xs[a, 2 * dx + 1]], axis=1)

    pass_on(1)
    pass_on_opposite(0)
    pass_on_opposite(1)
    for i in range(2):
        for d in (1, 3, 2):
            arrived(cut(wrows.at[d], i), wy_r.at[i, d]).wait_recv()
    for d in range(4):
        rows = pl.ds(pl.multiple_of(((y + d) % 4) * DY, 16), DY)
        wall[rows, 0 : 2 * HID] = load_gate_up(lambda t: wrows[d, t])
    for dx in (0, 1, 3, 2):
        cols = pl.ds(dx * 256, 256)
        wait_pair(0, dx)
        sums = tn(wall[:, 0 : 2 * HID], pair(0, dx))
        gate_sum, up_sum = sums[0:HID], sums[HID : 2 * HID]
        sig = jax.nn.sigmoid(gate_sum)
        swished = gate_sum * sig
        swi[:, cols] = swished
        slo[:, cols] = up_sum * sig * (1.0 + gate_sum * (1.0 - sig))
        hid[:, cols] = (swished * up_sum).astype(BF16)
    xy = {}
    for dx in (0, 1, 3, 2):
        wait_pair(1, dx)

    def spread(k, d, first, start, count):
        for dx in (2, 1, 3, 0):
            piece = ysend.at[d, pl.ds(first + start((x + dx) % 4), count)]
            there = ((4 - dx) % 4, (4 - d) % 4)
            place = pl.ds(0, count) if k == 0 else pl.ds(GU_WIDE, count)
            if d or dx:
                xy[dx, d, k] = rcopy(
                    piece, xyr.at[there[0], there[1], place], xy_s.at[k, dx, d], xy_r.at[k, there[0], there[1]],
                    dev(x + dx, y + d, z, c),
                )
                xy[dx, d, k].start()
            else:
                xyr[0, 0, place] = piece[...]

    def rows_of(a, d):
        rows = pl.ds(pl.multiple_of(((y + d) % 4) * DY, 16), DY)
        return jnp.concatenate([xs[a, s, rows, :] for s in range(8)], axis=1)

    for d in (2, 1, 3, 0):
        store_down(ysend.at[d], nt(rows_of(1, d), hid[...]).astype(BF16))
        spread(1, d, 27, down_start, DN_WIDE)
    for d in (1, 3, 2):
        arrived(cut(wrows.at[d], 2), wy_r.at[2, d]).wait_recv()
    for d in range(4):
        rows = pl.ds(pl.multiple_of(((y + d) % 4) * DY, 16), DY)
        wall[rows, 2 * HID : 3 * HID] = load_down(lambda t: wrows[d, t])
    for dx in (0, 1, 3, 2):
        cols = pl.ds(dx * 256, 256)
        grad_hidden = tn(wall[:, 2 * HID : 3 * HID], pair(1, dx))
        ggu[0:HID, cols] = (grad_hidden * slo[:, cols]).astype(BF16)
        ggu[HID : 2 * HID, cols] = (grad_hidden * swi[:, cols]).astype(BF16)
    for d in (2, 1, 3, 0):
        store_gate_up(ysend.at[d], nt(rows_of(0, d), ggu[...]).astype(BF16))
        spread(0, d, 0, gate_up_start, GU_WIDE)

    sib = {}
    for dx in (2, 1, 3, 0):
        cols = pl.ds(dx * 256, 256)
        for a in (0, 1):
            part = nn(wall[:, 2 * HID : 3 * HID], hid[:, cols]) if a == 0 else nn(wall[:, 0 : 2 * HID], ggu[:, cols])
            own[a, dx] = part[:, 0:ROWS]
            sib_out[a, dx] = part[:, ROWS : 2 * ROWS].astype(BF16)
            sib[a, dx] = rcopy(
                sib_out.at[a, dx], sib_in.at[a, dx], sib_s.at[a, dx], sib_r.at[a, dx], group(0, 1)
            )
            sib[a, dx].start()
    tr = {}
    tro = {}
    for a in (0, 1):
        sib[a, 2].wait_recv()
        xsend[a, 2] = (own[a, 2] + sib_in[a, 2].astype(F32)).astype(BF16)
        for dx in (1, 3):
            tro[a, dx] = rcopy(
                xsend.at[a, 2, halves[dx]], xopp.at[a, halves[dx]], tro_s.at[a, dx], tro_r.at[a, dx], group(dx, 0)
            )
            tro[a, dx].start()

    for dx in (0, 1, 3, 2):
        for d in (0, 1, 3, 2):
            for k, place in ((1, pl.ds(GU_WIDE, DN_WIDE)), (0, pl.ds(0, GU_WIDE))):
                if dx or d:
                    arrived(xyr.at[dx, d, place], xy_r.at[k, dx, d]).wait_recv()
    gz = {}
    keep = c == home
    for r in (3, 2, 1, 0):
        there = (r - x + 4) % 4
        total = xyr[there, 0].astype(F32)
        for d in (1, 2, 3):
            total = total + xyr[there, d].astype(F32)
        total = total.astype(BF16)
        zs[r, 0, 0:4] = total[0:4]
        zs[r, 0, 4:6] = total[7:9]
        zs[r, 1, 0:4] = total[3:7]
        zs[r, 1, 4:6] = total[9:11]
        slot = shift[r] + 4
        for h in range(2):
            gz[r, h] = rcopy(
                zs.at[r, h], zr.at[slot], gz_s.at[r, h], gz_r.at[slot], dev(x, y, z + shift[r], h)
            )
            if r:
                gz[r, h].start()
            else:
                stays = jnp.logical_and(keep, c == h)

                @pl.when(jnp.logical_not(stays))
                def _(h=h):
                    gz[0, h].start()

                @pl.when(stays)
                def _(h=h):
                    zr[4] = zs[0, h]

    for a in (0, 1):
        for dx in (1, 3):
            sib[a, dx].wait_recv()
            arrived(xopp.at[a, halves[dx]], tro_r.at[a, dx]).wait_recv()
            part = own[a, dx] + sib_in[a, dx].astype(F32)
            extra = xopp[a, halves[dx]].astype(F32)
            if dx == 1:
                part = jnp.concatenate([part[0 : D // 2] + extra, part[D // 2 : D]], axis=0)
            else:
                part = jnp.concatenate([part[0 : D // 2], part[D // 2 : D] + extra], axis=0)
            xsend[a, dx] = part.astype(BF16)
            tr[a, dx] = rcopy(
                xsend.at[a, dx], xrecv.at[a, 4 - dx], tr_s.at[a, dx], tr_r.at[a, 4 - dx], group(dx, 0)
            )
            tr[a, dx].start()

    total = None
    for s in (5, 3, 6, 2, 7, 1, 0):
        arrived(zr.at[s], gz_r.at[s]).wait_recv()

    @pl.when(jnp.logical_not(keep))
    def _():
        arrived(zr.at[4], gz_r.at[4]).wait_recv()

    total = zr[0].astype(F32)
    for s in range(1, 8):
        total = total + zr[s].astype(F32)
    zhsend[...] = total.astype(BF16)
    zhc = rcopy(zhsend, zhrecv, zh_s, zh_r, zh_dev)
    pl.semaphore_wait(far_sem, 1)
    zhc.start()

    for a, out in ((0, mixed_ref), (1, gtok_ref)):
        sib[a, 0].wait_recv()
        total = own[a, 0] + sib_in[a, 0].astype(F32)
        for dx in (1, 3):
            arrived(xrecv.at[a, dx], tr_r.at[a, dx]).wait_recv()
            total = total + xrecv[a, dx].astype(F32)
        out[...] = total.astype(BF16)

    zhc.wait()
    me = x * 2 + c
    fin[me] = (zhsend[...].astype(F32) + zhrecv[...].astype(F32)).astype(BF16)
    ag = {}
    for dx in (2, 1, 3, 0):
        for dc in (1, 0):
            if dx or dc:
                slot = ((4 - dx) % 4) * 2 + dc
                ag[dx, dc] = rcopy(fin.at[me], fin.at[me], ag_s.at[dx * 2 + dc], ag_r.at[slot], group(dx, dc))
                ag[dx, dc].start()
    for dx in range(4):
        for dc in range(2):
            if dx or dc:
                rank = ((x + dx) % 4) * 2 + (c if dc == 0 else sib_c)
                arrived(fin.at[rank], ag_r.at[dx * 2 + dc]).wait_recv()

    def summed(t):
        over = min(t // 7, 3) if t < 27 else min((t - 27) // 4, 3)
        u = t - gate_up_start(over) if t < 27 else t - 27 - down_start(over)
        if t < 27:
            half, u = (0, u) if u < 4 else (1, u - 3)
        else:
            half, u = u // 2, 4 + u % 2
        return fin[2 * over + half, u]

    whole = load_gate_up(summed)
    ggate_ref[...] = whole[:, 0:HID]
    gup_ref[...] = whole[:, HID : 2 * HID]
    gdown_ref[...] = load_down(summed)

    @pl.when(remote)
    def _():
        for cp in wz:
            cp.wait_send()

    for key, cp in gz.items():
        if key[0]:
            cp.wait_send()
        else:

            @pl.when(jnp.logical_not(jnp.logical_and(keep, c == key[1])))
            def _(cp=cp):
                cp.wait_send()

    for cps in (tok, opp, fwd, wy, xy, sib, tro, tr, ag):
        for cp in cps.values():
            cp.wait_send()


def place(*refs):
    for i, o in zip(refs[:5], refs[5:]):
        o[...] = i[...]


def per_device(tokens, gate_weight, up_weight, down_weight, cotangent):
    dma = pltpu.SemaphoreType.DMA
    vm = pltpu.VMEM
    outs = (
        jax.ShapeDtypeStruct((D, ROWS), BF16),
        jax.ShapeDtypeStruct((D, ROWS), BF16),
        jax.ShapeDtypeStruct((DY, HID), BF16),
        jax.ShapeDtypeStruct((DY, HID), BF16),
        jax.ShapeDtypeStruct((DY, HID), BF16),
    )
    pieces = len(CUTS) - 1
    results = pl.pallas_call(
        kernel,
        out_shape=outs,
        in_specs=[pl.BlockSpec(memory_space=pl.ANY)] * 5,
        out_specs=[pl.BlockSpec(memory_space=vm)] * 5,
        scratch_shapes=[
            vm((2, 8, D, ROWS), BF16),
            vm((3, DY, HID), BF16),
            vm((TILES, 16, 128), BF16),
            vm((4, TILES, 16, 128), BF16),
            vm((D, 3 * HID), BF16),
            vm((HID, 8 * ROWS), F32),
            vm((HID, 8 * ROWS), F32),
            vm((2 * HID, 8 * ROWS), BF16),
            vm((HID, 8 * ROWS), BF16),
            vm((2, 4, D, ROWS), BF16),
            vm((2, 4, D, ROWS), F32),
            vm((2, 4, D, ROWS), BF16),
            vm((2, 4, D, ROWS), BF16),
            vm((2, 4, D, ROWS), BF16),
            vm((2, D, ROWS), BF16),
            vm((4, TILES, 16, 128), BF16),
            vm((4, 4, GU_WIDE + DN_WIDE, 16, 128), BF16),
            vm((4, 2, HALF, 16, 128), BF16),
            vm((8, HALF, 16, 128), BF16),
            vm((HALF, 16, 128), BF16),
            vm((HALF, 16, 128), BF16),
            vm((8, HALF, 16, 128), BF16),
            dma((5,)),
            dma((2, 4)), dma((2, 4)),
            dma((2, 7)), dma((2, 7)),
            dma((pieces,)), dma((pieces,)),
            dma((pieces, 4)), dma((pieces, 4)),
            dma((2, 4)), dma((2, 4)),
            dma((2, 4)), dma((2, 4)),
            dma((2, 4)), dma((2, 4)),
            dma((2, 4)), dma((2, 4)),
            dma((2, 4, 4)), dma((2, 4, 4)),
            dma((4, 2)), dma((8,)),
            dma, dma,
            dma((8,)), dma((8,)),
            pltpu.SemaphoreType.REGULAR,
        ],
        compiler_params=pltpu.CompilerParams(
            collective_id=0, has_side_effects=True, vmem_limit_bytes=60 << 20
        ),
        name="swiglu",
    )(tokens.T, gate_weight, up_weight, down_weight.T, cotangent.T)
    mixed, gtok, ggate, gup, gdown = pl.pallas_call(
        place,
        out_shape=outs,
        in_specs=[pl.BlockSpec(memory_space=vm)] * 5,
        out_specs=[pl.BlockSpec(memory_space=vm)] * 5,
        name="place",
    )(*results)
    return mixed.T, gtok.T, ggate, gup, gdown.T


def solution(mesh):
    return jax.shard_map(
        per_device,
        mesh=mesh,
        in_specs=(
            P(("dp", "fsdp", "tensor"), None),
            P("fsdp", "tensor"),
            P("fsdp", "tensor"),
            P("tensor", "fsdp"),
            P(("dp", "fsdp", "tensor"), None),
        ),
        out_specs=(
            P(("dp", "fsdp", "tensor"), None),
            P(("dp", "fsdp", "tensor"), None),
            P("fsdp", "tensor"),
            P("fsdp", "tensor"),
            P("tensor", "fsdp"),
        ),
        check_vma=False,
    )
```

```python
import jax
import jax.numpy as jnp
from jax import lax
from jax.experimental import pallas as pl
from jax.experimental.pallas import tpu as pltpu
from jax.sharding import PartitionSpec as P

MESH = pl.DeviceIdType.MESH
F32 = jnp.float32
BF16 = jnp.bfloat16

D = 576
ROWS = 128
DY = 144
HID = 192
TILES = 41
CUTS = (0, 7, 14, 21, 27, 34, 41)
GU_CUTS = 4
GU_WIDE, DN_WIDE = 7, 4
HALF = 6


def gate_up_start(x):
    return 7 * x - x // 3


def down_start(x):
    return 4 * x - 2 * (x // 3)


def tn(left, right):
    return lax.dot_general(left, right, (((0,), (0,)), ((), ())), preferred_element_type=F32)


def nt(left, right):
    return lax.dot_general(left, right, (((1,), (1,)), ((), ())), preferred_element_type=F32)


def nn(left, right):
    return jnp.dot(left, right, preferred_element_type=F32)


def store_gate_up(ref, value):
    for r in range(9):
        for q in range(3):
            ref[3 * r + q] = value[16 * r : 16 * r + 16, 128 * q : 128 * q + 128]


def store_down(ref, value):
    for r in range(9):
        ref[27 + r] = value[16 * r : 16 * r + 16, 0:128]
    for i in range(4):
        ref[36 + i] = jnp.concatenate(
            [value[32 * i : 32 * i + 16, 128:192], value[32 * i + 16 : 32 * i + 32, 128:192]], axis=1
        )
    ref[40] = jnp.concatenate([value[128:144, 128:192], jnp.zeros((16, 64), value.dtype)], axis=1)


def load_gate_up(tile):
    return jnp.concatenate(
        [jnp.concatenate([tile(3 * r + q) for q in range(3)], axis=1) for r in range(9)], axis=0
    )


def load_down(tile):
    rows = []
    for r in range(9):
        last = tile(36 + r // 2)
        rows.append(jnp.concatenate([tile(27 + r), last[:, 0:64] if r % 2 == 0 else last[:, 64:128]], axis=1))
    return jnp.concatenate(rows, axis=0)


def kernel(
    tok_ref, gate_ref, up_ref, down_ref, cot_ref,
    mixed_ref, gtok_ref, ggate_ref, gup_ref, gdown_ref,
    xs, win, wmine, wrows, wall, swi, slo, ggu, hid, sib_out, own, sib_in, xsend, xrecv, xopp,
    ysend, xyr, zs, zr, zhsend, zhrecv, fin,
    in_s, tok_s, tok_r, fwd_s, fwd_r, wz_s, wz_r, wy_s, wy_r, opp_s, opp_r,
    sib_s, sib_r, tro_s, tro_r, tr_s, tr_r, xy_s, xy_r, gz_s, gz_r, zh_s, zh_r, ag_s, ag_r, far_sem,
):
    dp = lax.axis_index("dp")
    y = lax.axis_index("fsdp")
    zl = lax.axis_index("tensor")
    x, zh, c = dp // 4, (dp // 2) % 2, dp % 2
    z = zh * 8 + zl
    sib_c = 1 - c
    home = zl // 4

    def dev(xx, yy, zz, cc):
        zz = (zz + 16) % 16
        return (((xx + 4) % 4) * 4 + (zz // 8) * 2 + cc, (yy + 4) % 4, zz % 8)

    def group(dx, dc):
        return dev(x + dx, y, z, c if dc == 0 else sib_c)

    k_to = (c + home) % 2
    local = jnp.logical_and(x == 0, k_to == 0)
    remote = jnp.logical_not(local)
    zh_dev = dev(x, y, z + 8, c)

    def z_to(i):
        return dev(x, y, z + jnp.where(x == 0, 4 - 8 * (i % 2), 4 * k_to - x), home)


    shift = [jnp.where(((zl + r) % 4 + 4 * c - zl + 8) % 8 == r, r, r - 4) for r in range(4)]

    def rcopy(src, dst, ssem, rsem, to):
        return pltpu.make_async_remote_copy(
            src_ref=src, dst_ref=dst, send_sem=ssem, recv_sem=rsem, device_id=to, device_id_type=MESH
        )

    inputs = [
        pltpu.make_async_copy(tok_ref, xs.at[0, 0], in_s.at[0]),
        pltpu.make_async_copy(cot_ref, xs.at[1, 0], in_s.at[1]),
        pltpu.make_async_copy(gate_ref, win.at[0], in_s.at[2]),
        pltpu.make_async_copy(up_ref, win.at[1], in_s.at[3]),
        pltpu.make_async_copy(down_ref, win.at[2], in_s.at[4]),
    ]
    for cp in inputs:
        cp.start()

    barrier = pltpu.get_barrier_semaphore()

    def greet(to):
        pl.semaphore_signal(barrier, inc=1, device_id=to, device_id_type=MESH)

    for s in (4, -4):
        for h in range(2):
            greet(dev(x, y, z + s, h))
    for s in (3, -3, 2, -2, 1, -1):
        greet(dev(x, y, z - s, home))
    for r in (3, 2, 1):
        for h in range(2):
            greet(dev(x, y, z + shift[r], h))
    for dx in (2, 1, 3, 0):
        for d in (2, 1, 3, 0):
            if dx or d:
                greet(dev(x + dx, y + d, z, c))
        greet(group(dx, 1))

    for cp in inputs:
        cp.wait()
    store_gate_up(wmine, jnp.concatenate([win[0], win[1]], axis=1))
    store_down(wmine, win[2])

    pl.semaphore_wait(barrier, 35)

    pl.semaphore_signal(far_sem, inc=1, device_id=dev(x, y, z - 4, c), device_id_type=MESH)

    def cut(ref, i):
        return ref.at[pl.ds(CUTS[i], CUTS[i + 1] - CUTS[i])]

    wz = [
        rcopy(cut(wmine, i), cut(wrows.at[0], i), wz_s.at[i], wz_r.at[i], z_to(i)) for i in range(len(CUTS) - 1)
    ]

    @pl.when(remote)
    def _():
        for cp in wz:
            cp.start()

    tok = {}
    opp = {}
    fwd = {}
    halves = {1: pl.ds(0, D // 2), 3: pl.ds(D // 2, D // 2)}
    for a in (0, 1):
        for dx in (1, 3):
            tok[a, dx] = rcopy(
                xs.at[a, 0], xs.at[a, 2 * (4 - dx)], tok_s.at[a, dx], tok_r.at[a, 4 - dx], group(dx, 0)
            )
            tok[a, dx].start()
    for a in (0, 1):
        fwd[a, 0] = rcopy(xs.at[a, 0], xs.at[a, 1], fwd_s.at[a, 0], fwd_r.at[a, 0], group(0, 1))
        fwd[a, 0].start()

    @pl.when(local)
    def _():
        wrows[0] = wmine[...]

    def arrived(ref, sem):
        return rcopy(ref, ref, sem, sem, group(0, 1))

    def pass_on(a):
        for dx in (1, 3):
            arrived(xs.at[a, 2 * dx], tok_r.at[a, dx]).wait_recv()
            opp[a, dx] = rcopy(
                xs.at[a, 2 * dx, halves[dx]], xs.at[a, 4, halves[dx]], opp_s.at[a, dx], opp_r.at[a, dx],
                group(4 - dx, 0),
            )
            opp[a, dx].start()
            fwd[a, dx] = rcopy(
                xs.at[a, 2 * dx], xs.at[a, 2 * dx + 1], fwd_s.at[a, dx], fwd_r.at[a, dx], group(0, 1)
            )
            fwd[a, dx].start()

    def pass_on_opposite(a):
        for dx in (1, 3):
            arrived(xs.at[a, 4, halves[dx]], opp_r.at[a, dx]).wait_recv()
            fwd[a, dx + 3] = rcopy(
                xs.at[a, 4, halves[dx]], xs.at[a, 5, halves[dx]], fwd_s.at[a, dx + 3], fwd_r.at[a, dx + 3], group(0, 1)
            )
            fwd[a, dx + 3].start()

    def wait_pair(a, dx):
        for k in (dx,) if dx != 2 else (4, 6):
            fwd[a, k].wait_recv()

    wy = {}

    for i in range(len(CUTS) - 1):

        @pl.when(remote)
        def _(i=i):
            wz[i].wait_recv()

        for d in (2, 1, 3):
            wy[i, d] = rcopy(
                cut(wrows.at[0], i), cut(wrows.at[4 - d], i), wy_s.at[i, d], wy_r.at[i, 4 - d],
                dev(x, y + d, z, c),
            )
            wy[i, d].start()
        if i == 1:
            pass_on(0)
        if i == 4:
            pass_on(1)

    def pair(a, dx):
        return jnp.concatenate([xs[a, 2 * dx], xs[a, 2 * dx + 1]], axis=1)

    pass_on_opposite(0)
    for i in range(GU_CUTS):
        for d in (1, 3, 2):
            arrived(cut(wrows.at[d], i), wy_r.at[i, d]).wait_recv()
    for d in range(4):
        rows = pl.ds(pl.multiple_of(((y + d) % 4) * DY, 16), DY)
        wall[rows, 0 : 2 * HID] = load_gate_up(lambda t: wrows[d, t])
    for dx in (0, 1, 3, 2):
        if dx == 2:
            pass_on_opposite(1)
        cols = pl.ds(dx * 256, 256)
        wait_pair(0, dx)
        sums = tn(wall[:, 0 : 2 * HID], pair(0, dx))
        gate_sum, up_sum = sums[0:HID], sums[HID : 2 * HID]
        sig = jax.nn.sigmoid(gate_sum)
        swished = gate_sum * sig
        swi[:, cols] = swished
        slo[:, cols] = up_sum * sig * (1.0 + gate_sum * (1.0 - sig))
        hid[:, cols] = (swished * up_sum).astype(BF16)
    xy = {}
    for dx in (0, 1, 3, 2):
        wait_pair(1, dx)

    def spread(k, d, first, start, count):
        for dx in (2, 1, 3, 0):
            piece = ysend.at[d, pl.ds(first + start((x + dx) % 4), count)]
            there = ((4 - dx) % 4, (4 - d) % 4)
            place = pl.ds(0, count) if k == 0 else pl.ds(GU_WIDE, count)
            if d or dx:
                xy[dx, d, k] = rcopy(
                    piece, xyr.at[there[0], there[1], place], xy_s.at[k, dx, d], xy_r.at[k, there[0], there[1]],
                    dev(x + dx, y + d, z, c),
                )
                xy[dx, d, k].start()
            else:
                xyr[0, 0, place] = piece[...]

    def rows_of(a, d):
        rows = pl.ds(pl.multiple_of(((y + d) % 4) * DY, 16), DY)
        return jnp.concatenate([xs[a, s, rows, :] for s in range(8)], axis=1)

    for d in (2, 1, 3, 0):
        store_down(ysend.at[d], nt(rows_of(1, d), hid[...]).astype(BF16))
        spread(1, d, 27, down_start, DN_WIDE)
    for i in range(GU_CUTS, len(CUTS) - 1):
        for d in (1, 3, 2):
            arrived(cut(wrows.at[d], i), wy_r.at[i, d]).wait_recv()
    for d in range(4):
        rows = pl.ds(pl.multiple_of(((y + d) % 4) * DY, 16), DY)
        wall[rows, 2 * HID : 3 * HID] = load_down(lambda t: wrows[d, t])
    for dx in (0, 1, 3, 2):
        cols = pl.ds(dx * 256, 256)
        grad_hidden = tn(wall[:, 2 * HID : 3 * HID], pair(1, dx))
        ggu[0:HID, cols] = (grad_hidden * slo[:, cols]).astype(BF16)
        ggu[HID : 2 * HID, cols] = (grad_hidden * swi[:, cols]).astype(BF16)
    for d in (2, 1, 3, 0):
        store_gate_up(ysend.at[d], nt(rows_of(0, d), ggu[...]).astype(BF16))
        spread(0, d, 0, gate_up_start, GU_WIDE)

    sib = {}
    for dx in (2, 1, 3, 0):
        cols = pl.ds(dx * 256, 256)
        for a in (0, 1):
            part = nn(wall[:, 2 * HID : 3 * HID], hid[:, cols]) if a == 0 else nn(wall[:, 0 : 2 * HID], ggu[:, cols])
            own[a, dx] = part[:, 0:ROWS]
            sib_out[a, dx] = part[:, ROWS : 2 * ROWS].astype(BF16)
            sib[a, dx] = rcopy(
                sib_out.at[a, dx], sib_in.at[a, dx], sib_s.at[a, dx], sib_r.at[a, dx], group(0, 1)
            )
            sib[a, dx].start()
    tr = {}
    tro = {}
    for a in (0, 1):
        sib[a, 2].wait_recv()
        xsend[a, 2] = (own[a, 2] + sib_in[a, 2].astype(F32)).astype(BF16)
        for dx in (1, 3):
            tro[a, dx] = rcopy(
                xsend.at[a, 2, halves[dx]], xopp.at[a, halves[dx]], tro_s.at[a, dx], tro_r.at[a, dx], group(dx, 0)
            )
            tro[a, dx].start()

    for dx in (0, 1, 3, 2):
        for d in (0, 1, 3, 2):
            for k, place in ((1, pl.ds(GU_WIDE, DN_WIDE)), (0, pl.ds(0, GU_WIDE))):
                if dx or d:
                    arrived(xyr.at[dx, d, place], xy_r.at[k, dx, d]).wait_recv()
    gz = {}
    keep = c == home
    for r in (0, 3, 1, 2):
        there = (r - x + 4) % 4
        total = xyr[there, 0].astype(F32)
        for d in (1, 2, 3):
            total = total + xyr[there, d].astype(F32)
        total = total.astype(BF16)
        zs[r, 0, 0:4] = total[0:4]
        zs[r, 0, 4:6] = total[7:9]
        zs[r, 1, 0:4] = total[3:7]
        zs[r, 1, 4:6] = total[9:11]
        slot = shift[r] + 4
        for h in range(2):
            far = jnp.where(shift[r] == -4, 4 - 8 * h, shift[r])
            gz[r, h] = rcopy(
                zs.at[r, h], zr.at[slot], gz_s.at[r, h], gz_r.at[slot], dev(x, y, z + far, h)
            )
            if r:
                gz[r, h].start()
            else:
                stays = jnp.logical_and(keep, c == h)

                @pl.when(jnp.logical_not(stays))
                def _(h=h):
                    gz[0, h].start()

                @pl.when(stays)
                def _(h=h):
                    zr[4] = zs[0, h]

    for a in (0, 1):
        for dx in (1, 3):
            sib[a, dx].wait_recv()
            arrived(xopp.at[a, halves[dx]], tro_r.at[a, dx]).wait_recv()
            part = own[a, dx] + sib_in[a, dx].astype(F32)
            extra = xopp[a, halves[dx]].astype(F32)
            if dx == 1:
                part = jnp.concatenate([part[0 : D // 2] + extra, part[D // 2 : D]], axis=0)
            else:
                part = jnp.concatenate([part[0 : D // 2], part[D // 2 : D] + extra], axis=0)
            xsend[a, dx] = part.astype(BF16)
            tr[a, dx] = rcopy(
                xsend.at[a, dx], xrecv.at[a, 4 - dx], tr_s.at[a, dx], tr_r.at[a, 4 - dx], group(dx, 0)
            )
            tr[a, dx].start()

    total = None
    for s in (5, 3, 6, 2, 7, 1, 0):
        arrived(zr.at[s], gz_r.at[s]).wait_recv()

    @pl.when(jnp.logical_not(keep))
    def _():
        arrived(zr.at[4], gz_r.at[4]).wait_recv()

    total = zr[0].astype(F32)
    for s in range(1, 8):
        total = total + zr[s].astype(F32)
    zhsend[...] = total.astype(BF16)
    zhc = rcopy(zhsend, zhrecv, zh_s, zh_r, zh_dev)
    pl.semaphore_wait(far_sem, 1)
    zhc.start()

    for a, out in ((0, mixed_ref), (1, gtok_ref)):
        sib[a, 0].wait_recv()
        total = own[a, 0] + sib_in[a, 0].astype(F32)
        for dx in (1, 3):
            arrived(xrecv.at[a, dx], tr_r.at[a, dx]).wait_recv()
            total = total + xrecv[a, dx].astype(F32)
        out[...] = total.astype(BF16)

    zhc.wait()
    me = x * 2 + c
    fin[me] = (zhsend[...].astype(F32) + zhrecv[...].astype(F32)).astype(BF16)
    ag = {}
    for dx in (2, 1, 3, 0):
        for dc in (1, 0):
            if dx or dc:
                slot = ((4 - dx) % 4) * 2 + dc
                ag[dx, dc] = rcopy(fin.at[me], fin.at[me], ag_s.at[dx * 2 + dc], ag_r.at[slot], group(dx, dc))
                ag[dx, dc].start()
    for dx in range(4):
        for dc in range(2):
            if dx or dc:
                rank = ((x + dx) % 4) * 2 + (c if dc == 0 else sib_c)
                arrived(fin.at[rank], ag_r.at[dx * 2 + dc]).wait_recv()

    def summed(t):
        over = min(t // 7, 3) if t < 27 else min((t - 27) // 4, 3)
        u = t - gate_up_start(over) if t < 27 else t - 27 - down_start(over)
        if t < 27:
            half, u = (0, u) if u < 4 else (1, u - 3)
        else:
            half, u = u // 2, 4 + u % 2
        return fin[2 * over + half, u]

    whole = load_gate_up(summed)
    ggate_ref[...] = whole[:, 0:HID]
    gup_ref[...] = whole[:, HID : 2 * HID]
    gdown_ref[...] = load_down(summed)

    @pl.when(remote)
    def _():
        for cp in wz:
            cp.wait_send()

    for key, cp in gz.items():
        if key[0]:
            cp.wait_send()
        else:

            @pl.when(jnp.logical_not(jnp.logical_and(keep, c == key[1])))
            def _(cp=cp):
                cp.wait_send()

    for cps in (tok, opp, fwd, wy, xy, sib, tro, tr, ag):
        for cp in cps.values():
            cp.wait_send()


def place(*refs):
    for i, o in zip(refs[:5], refs[5:]):
        o[...] = i[...]


def per_device(tokens, gate_weight, up_weight, down_weight, cotangent):
    dma = pltpu.SemaphoreType.DMA
    vm = pltpu.VMEM
    outs = (
        jax.ShapeDtypeStruct((D, ROWS), BF16),
        jax.ShapeDtypeStruct((D, ROWS), BF16),
        jax.ShapeDtypeStruct((DY, HID), BF16),
        jax.ShapeDtypeStruct((DY, HID), BF16),
        jax.ShapeDtypeStruct((DY, HID), BF16),
    )
    pieces = len(CUTS) - 1
    results = pl.pallas_call(
        kernel,
        out_shape=outs,
        in_specs=[pl.BlockSpec(memory_space=pl.ANY)] * 5,
        out_specs=[pl.BlockSpec(memory_space=vm)] * 5,
        scratch_shapes=[
            vm((2, 8, D, ROWS), BF16),
            vm((3, DY, HID), BF16),
            vm((TILES, 16, 128), BF16),
            vm((4, TILES, 16, 128), BF16),
            vm((D, 3 * HID), BF16),
            vm((HID, 8 * ROWS), F32),
            vm((HID, 8 * ROWS), F32),
            vm((2 * HID, 8 * ROWS), BF16),
            vm((HID, 8 * ROWS), BF16),
            vm((2, 4, D, ROWS), BF16),
            vm((2, 4, D, ROWS), F32),
            vm((2, 4, D, ROWS), BF16),
            vm((2, 4, D, ROWS), BF16),
            vm((2, 4, D, ROWS), BF16),
            vm((2, D, ROWS), BF16),
            vm((4, TILES, 16, 128), BF16),
            vm((4, 4, GU_WIDE + DN_WIDE, 16, 128), BF16),
            vm((4, 2, HALF, 16, 128), BF16),
            vm((8, HALF, 16, 128), BF16),
            vm((HALF, 16, 128), BF16),
            vm((HALF, 16, 128), BF16),
            vm((8, HALF, 16, 128), BF16),
            dma((5,)),
            dma((2, 4)), dma((2, 4)),
            dma((2, 7)), dma((2, 7)),
            dma((pieces,)), dma((pieces,)),
            dma((pieces, 4)), dma((pieces, 4)),
            dma((2, 4)), dma((2, 4)),
            dma((2, 4)), dma((2, 4)),
            dma((2, 4)), dma((2, 4)),
            dma((2, 4)), dma((2, 4)),
            dma((2, 4, 4)), dma((2, 4, 4)),
            dma((4, 2)), dma((8,)),
            dma, dma,
            dma((8,)), dma((8,)),
            pltpu.SemaphoreType.REGULAR,
        ],
        compiler_params=pltpu.CompilerParams(
            collective_id=0, has_side_effects=True, vmem_limit_bytes=60 << 20
        ),
        name="swiglu",
    )(tokens.T, gate_weight, up_weight, down_weight.T, cotangent.T)
    mixed, gtok, ggate, gup, gdown = pl.pallas_call(
        place,
        out_shape=outs,
        in_specs=[pl.BlockSpec(memory_space=vm)] * 5,
        out_specs=[pl.BlockSpec(memory_space=vm)] * 5,
        name="place",
    )(*results)
    return mixed.T, gtok.T, ggate, gup, gdown.T


def solution(mesh):
    return jax.shard_map(
        per_device,
        mesh=mesh,
        in_specs=(
            P(("dp", "fsdp", "tensor"), None),
            P("fsdp", "tensor"),
            P("fsdp", "tensor"),
            P("tensor", "fsdp"),
            P(("dp", "fsdp", "tensor"), None),
        ),
        out_specs=(
            P(("dp", "fsdp", "tensor"), None),
            P(("dp", "fsdp", "tensor"), None),
            P("fsdp", "tensor"),
            P("fsdp", "tensor"),
            P("tensor", "fsdp"),
        ),
        check_vma=False,
    )
```

```python
import jax
import jax.numpy as jnp
from jax import lax
from jax.experimental import pallas as pl
from jax.experimental.pallas import tpu as pltpu
from jax.sharding import PartitionSpec as P

MESH = pl.DeviceIdType.MESH
F32 = jnp.float32
BF16 = jnp.bfloat16

D = 576
ROWS = 128
DY = 144
HID = 192
TILES = 41
CUTS = (0, 7, 14, 21, 27, 34, 41)
GU_CUTS = 4
FIRST = (27, 0, 15)
WIDE = (4, 4, 3)
PLACE = (0, 4, 8)
SPLIT = 80
PARTS = (0, 1, 2)


def start_of(part, x):
    return (4 * x - 2 * (x // 3), 4 * x - x // 3, 3 * x)[part]


def core_start(part, core):
    return (2 * core, 2 * core, core)[part]


def tn(left, right):
    return lax.dot_general(left, right, (((0,), (0,)), ((), ())), preferred_element_type=F32)


def nt(left, right):
    return lax.dot_general(left, right, (((1,), (1,)), ((), ())), preferred_element_type=F32)


def nn(left, right):
    return jnp.dot(left, right, preferred_element_type=F32)


def store_gate_up(ref, value, row=0):
    for r in range(value.shape[0] // 16):
        for q in range(3):
            ref[3 * (r + row) + q] = value[16 * r : 16 * r + 16, 128 * q : 128 * q + 128]


def store_down(ref, value):
    for r in range(9):
        ref[27 + r] = value[16 * r : 16 * r + 16, 0:128]
    for i in range(4):
        ref[36 + i] = jnp.concatenate(
            [value[32 * i : 32 * i + 16, 128:192], value[32 * i + 16 : 32 * i + 32, 128:192]], axis=1
        )
    ref[40] = jnp.concatenate([value[128:144, 128:192], jnp.zeros((16, 64), value.dtype)], axis=1)


def load_gate_up(tile):
    return jnp.concatenate(
        [jnp.concatenate([tile(3 * r + q) for q in range(3)], axis=1) for r in range(9)], axis=0
    )


def load_down(tile):
    rows = []
    for r in range(9):
        last = tile(36 + r // 2)
        rows.append(jnp.concatenate([tile(27 + r), last[:, 0:64] if r % 2 == 0 else last[:, 64:128]], axis=1))
    return jnp.concatenate(rows, axis=0)


def kernel(
    tok_ref, gate_ref, up_ref, down_ref, cot_ref,
    mixed_ref, gtok_ref, ggate_ref, gup_ref, gdown_ref,
    xs, win, wmine, wrows, wall, swi, slo, ggu, hid, sib_out, own, sib_in, xsend, xrecv, xopp,
    ysend, xyr, zs, zr, zhsend, zhrecv, fin,
    in_s, tok_s, tok_r, fwd_s, fwd_r, wz_s, wz_r, wy_s, wy_r, opp_s, opp_r,
    sib_s, sib_r, tro_s, tro_r, tr_s, tr_r, xy_s, xy_r, gz_s, gz_r, zh_s, zh_r, ag_s, ag_r, far_sem,
):
    dp = lax.axis_index("dp")
    y = lax.axis_index("fsdp")
    zl = lax.axis_index("tensor")
    x, zh, c = dp // 4, (dp // 2) % 2, dp % 2
    z = zh * 8 + zl
    sib_c = 1 - c
    home = zl // 4

    def dev(xx, yy, zz, cc):
        zz = (zz + 16) % 16
        return (((xx + 4) % 4) * 4 + (zz // 8) * 2 + cc, (yy + 4) % 4, zz % 8)

    def group(dx, dc):
        return dev(x + dx, y, z, c if dc == 0 else sib_c)

    k_to = (c + home) % 2
    local = jnp.logical_and(x == 0, k_to == 0)
    remote = jnp.logical_not(local)
    zh_dev = dev(x, y, z + 8, c)

    def z_to(i):
        return dev(x, y, z + jnp.where(x == 0, 4 - 8 * (i % 2), 4 * k_to - x), home)


    shift = [jnp.where(((zl + r) % 4 + 4 * c - zl + 8) % 8 == r, r, r - 4) for r in range(4)]

    def rcopy(src, dst, ssem, rsem, to):
        return pltpu.make_async_remote_copy(
            src_ref=src, dst_ref=dst, send_sem=ssem, recv_sem=rsem, device_id=to, device_id_type=MESH
        )

    inputs = [
        pltpu.make_async_copy(tok_ref, xs.at[0, 0], in_s.at[0]),
        pltpu.make_async_copy(cot_ref, xs.at[1, 0], in_s.at[1]),
        pltpu.make_async_copy(gate_ref, win.at[0], in_s.at[2]),
        pltpu.make_async_copy(up_ref, win.at[1], in_s.at[3]),
        pltpu.make_async_copy(down_ref, win.at[2], in_s.at[4]),
    ]
    for cp in inputs:
        cp.start()

    barrier = pltpu.get_barrier_semaphore()

    def greet(to):
        pl.semaphore_signal(barrier, inc=1, device_id=to, device_id_type=MESH)

    for s in (4, -4):
        for h in range(2):
            greet(dev(x, y, z + s, h))
    for s in (3, -3, 2, -2, 1, -1):
        greet(dev(x, y, z - s, home))
    for r in (3, 2, 1):
        for h in range(2):
            greet(dev(x, y, z + shift[r], h))
    for dx in (2, 1, 3, 0):
        for d in (2, 1, 3, 0):
            if dx or d:
                greet(dev(x + dx, y + d, z, c))
        greet(group(dx, 1))

    for cp in inputs:
        cp.wait()
    store_gate_up(wmine, jnp.concatenate([win[0], win[1]], axis=1))
    store_down(wmine, win[2])

    pl.semaphore_wait(barrier, 35)

    pl.semaphore_signal(far_sem, inc=1, device_id=dev(x, y, z - 4, c), device_id_type=MESH)

    def cut(ref, i):
        return ref.at[pl.ds(CUTS[i], CUTS[i + 1] - CUTS[i])]

    wz = [
        rcopy(cut(wmine, i), cut(wrows.at[0], i), wz_s.at[i], wz_r.at[i], z_to(i)) for i in range(len(CUTS) - 1)
    ]

    @pl.when(remote)
    def _():
        for cp in wz:
            cp.start()

    tok = {}
    opp = {}
    fwd = {}
    halves = {1: pl.ds(0, D // 2), 3: pl.ds(D // 2, D // 2)}
    for a in (0, 1):
        for dx in (1, 3):
            tok[a, dx] = rcopy(
                xs.at[a, 0], xs.at[a, 2 * (4 - dx)], tok_s.at[a, dx], tok_r.at[a, 4 - dx], group(dx, 0)
            )
            tok[a, dx].start()
    for a in (0, 1):
        fwd[a, 0] = rcopy(xs.at[a, 0], xs.at[a, 1], fwd_s.at[a, 0], fwd_r.at[a, 0], group(0, 1))
        fwd[a, 0].start()

    @pl.when(local)
    def _():
        wrows[0] = wmine[...]

    def arrived(ref, sem):
        return rcopy(ref, ref, sem, sem, group(0, 1))

    def pass_on(a):
        for dx in (1, 3):
            arrived(xs.at[a, 2 * dx], tok_r.at[a, dx]).wait_recv()
            opp[a, dx] = rcopy(
                xs.at[a, 2 * dx, halves[dx]], xs.at[a, 4, halves[dx]], opp_s.at[a, dx], opp_r.at[a, dx],
                group(4 - dx, 0),
            )
            opp[a, dx].start()
            fwd[a, dx] = rcopy(
                xs.at[a, 2 * dx], xs.at[a, 2 * dx + 1], fwd_s.at[a, dx], fwd_r.at[a, dx], group(0, 1)
            )
            fwd[a, dx].start()

    def pass_on_opposite(a):
        for dx in (1, 3):
            arrived(xs.at[a, 4, halves[dx]], opp_r.at[a, dx]).wait_recv()
            fwd[a, dx + 3] = rcopy(
                xs.at[a, 4, halves[dx]], xs.at[a, 5, halves[dx]], fwd_s.at[a, dx + 3], fwd_r.at[a, dx + 3], group(0, 1)
            )
            fwd[a, dx + 3].start()

    def wait_pair(a, dx):
        for k in (dx,) if dx != 2 else (4, 6):
            fwd[a, k].wait_recv()

    wy = {}

    for i in range(len(CUTS) - 1):

        @pl.when(remote)
        def _(i=i):
            wz[i].wait_recv()

        for d in (2, 1, 3):
            wy[i, d] = rcopy(
                cut(wrows.at[0], i), cut(wrows.at[4 - d], i), wy_s.at[i, d], wy_r.at[i, 4 - d],
                dev(x, y + d, z, c),
            )
            wy[i, d].start()
        if i == 1:
            pass_on(0)
        if i == 4:
            pass_on(1)

    def pair(a, dx):
        return jnp.concatenate([xs[a, 2 * dx], xs[a, 2 * dx + 1]], axis=1)

    pass_on_opposite(0)
    for i in range(GU_CUTS):
        for d in (1, 3, 2):
            arrived(cut(wrows.at[d], i), wy_r.at[i, d]).wait_recv()
    for d in range(4):
        rows = pl.ds(pl.multiple_of(((y + d) % 4) * DY, 16), DY)
        wall[rows, 0 : 2 * HID] = load_gate_up(lambda t: wrows[d, t])
    for dx in (0, 1, 3, 2):
        if dx == 2:
            pass_on_opposite(1)
        cols = pl.ds(dx * 256, 256)
        wait_pair(0, dx)
        sums = tn(wall[:, 0 : 2 * HID], pair(0, dx))
        gate_sum, up_sum = sums[0:HID], sums[HID : 2 * HID]
        sig = jax.nn.sigmoid(gate_sum)
        swished = gate_sum * sig
        swi[:, cols] = swished
        slo[:, cols] = up_sum * sig * (1.0 + gate_sum * (1.0 - sig))
        hid[:, cols] = (swished * up_sum).astype(BF16)
    xy = {}
    for dx in (0, 1, 3, 2):
        wait_pair(1, dx)

    def spread(p, d):
        for dx in (2, 1, 3, 0):
            piece = ysend.at[d, pl.ds(FIRST[p] + start_of(p, (x + dx) % 4), WIDE[p])]
            there = ((4 - dx) % 4, (4 - d) % 4)
            place = pl.ds(PLACE[p], WIDE[p])
            if d or dx:
                xy[p, dx, d] = rcopy(
                    piece, xyr.at[there[0], there[1], place], xy_s.at[p, dx, d], xy_r.at[p, there[0], there[1]],
                    dev(x + dx, y + d, z, c),
                )
                xy[p, dx, d].start()
            else:
                xyr[0, 0, place] = piece[...]

    def rows_of(a, d, row=0, count=DY):
        rows = pl.ds(pl.multiple_of(((y + d) % 4) * DY + row, 16), count)
        return jnp.concatenate([xs[a, s, rows, :] for s in range(8)], axis=1)

    for d in (2, 1, 3, 0):
        store_down(ysend.at[d], nt(rows_of(1, d), hid[...]).astype(BF16))
        spread(0, d)
    for i in range(GU_CUTS, len(CUTS) - 1):
        for d in (1, 3, 2):
            arrived(cut(wrows.at[d], i), wy_r.at[i, d]).wait_recv()
    for d in range(4):
        rows = pl.ds(pl.multiple_of(((y + d) % 4) * DY, 16), DY)
        wall[rows, 2 * HID : 3 * HID] = load_down(lambda t: wrows[d, t])
    for dx in (0, 1, 3, 2):
        cols = pl.ds(dx * 256, 256)
        grad_hidden = tn(wall[:, 2 * HID : 3 * HID], pair(1, dx))
        ggu[0:HID, cols] = (grad_hidden * slo[:, cols]).astype(BF16)
        ggu[HID : 2 * HID, cols] = (grad_hidden * swi[:, cols]).astype(BF16)
    for d in (2, 1, 3, 0):
        store_gate_up(ysend.at[d], nt(rows_of(0, d, 0, SPLIT), ggu[...]).astype(BF16))
        spread(1, d)
    for d in (2, 1, 3, 0):
        store_gate_up(ysend.at[d], nt(rows_of(0, d, SPLIT, DY - SPLIT), ggu[...]).astype(BF16), SPLIT // 16)
        spread(2, d)

    sib = {}
    for dx in (2, 1, 3, 0):
        cols = pl.ds(dx * 256, 256)
        for a in (0, 1):
            part = nn(wall[:, 2 * HID : 3 * HID], hid[:, cols]) if a == 0 else nn(wall[:, 0 : 2 * HID], ggu[:, cols])
            own[a, dx] = part[:, 0:ROWS]
            sib_out[a, dx] = part[:, ROWS : 2 * ROWS].astype(BF16)
            sib[a, dx] = rcopy(
                sib_out.at[a, dx], sib_in.at[a, dx], sib_s.at[a, dx], sib_r.at[a, dx], group(0, 1)
            )
            sib[a, dx].start()
    tr = {}
    tro = {}
    for a in (0, 1):
        sib[a, 2].wait_recv()
        xsend[a, 2] = (own[a, 2] + sib_in[a, 2].astype(F32)).astype(BF16)
        for dx in (1, 3):
            tro[a, dx] = rcopy(
                xsend.at[a, 2, halves[dx]], xopp.at[a, halves[dx]], tro_s.at[a, dx], tro_r.at[a, dx], group(dx, 0)
            )
            tro[a, dx].start()

    gz = {}
    keep = c == home
    for p in PARTS:
        for dx in (0, 1, 3, 2):
            for d in (0, 1, 3, 2):
                if dx or d:
                    arrived(xyr.at[dx, d, pl.ds(PLACE[p], WIDE[p])], xy_r.at[p, dx, d]).wait_recv()
        for r in (0, 3, 1, 2):
            there = (r - x + 4) % 4
            total = xyr[there, 0, PLACE[p] : PLACE[p] + WIDE[p]].astype(F32)
            for d in (1, 2, 3):
                total = total + xyr[there, d, PLACE[p] : PLACE[p] + WIDE[p]].astype(F32)
            total = total.astype(BF16)
            slot = shift[r] + 4
            for h in range(2):
                zs[p, r, h] = total[core_start(p, h) : core_start(p, h) + 2]
                far = jnp.where(shift[r] == -4, 4 - 8 * h, shift[r])
                gz[p, r, h] = rcopy(
                    zs.at[p, r, h], zr.at[p, slot], gz_s.at[p, r, h], gz_r.at[p, slot], dev(x, y, z + far, h)
                )
                if r:
                    gz[p, r, h].start()
                else:
                    stays = jnp.logical_and(keep, c == h)

                    @pl.when(jnp.logical_not(stays))
                    def _(p=p, h=h):
                        gz[p, 0, h].start()

                    @pl.when(stays)
                    def _(p=p, h=h):
                        zr[p, 4] = zs[p, 0, h]

    for a in (0, 1):
        for dx in (1, 3):
            sib[a, dx].wait_recv()
            arrived(xopp.at[a, halves[dx]], tro_r.at[a, dx]).wait_recv()
            part = own[a, dx] + sib_in[a, dx].astype(F32)
            extra = xopp[a, halves[dx]].astype(F32)
            if dx == 1:
                part = jnp.concatenate([part[0 : D // 2] + extra, part[D // 2 : D]], axis=0)
            else:
                part = jnp.concatenate([part[0 : D // 2], part[D // 2 : D] + extra], axis=0)
            xsend[a, dx] = part.astype(BF16)
            tr[a, dx] = rcopy(
                xsend.at[a, dx], xrecv.at[a, 4 - dx], tr_s.at[a, dx], tr_r.at[a, 4 - dx], group(dx, 0)
            )
            tr[a, dx].start()

    pl.semaphore_wait(far_sem, 1)
    zhc = {}
    for p in PARTS:
        for s in (5, 3, 6, 2, 7, 1, 0):
            arrived(zr.at[p, s], gz_r.at[p, s]).wait_recv()

        @pl.when(jnp.logical_not(keep))
        def _(p=p):
            arrived(zr.at[p, 4], gz_r.at[p, 4]).wait_recv()

        total = zr[p, 0].astype(F32)
        for s in range(1, 8):
            total = total + zr[p, s].astype(F32)
        zhsend[p] = total.astype(BF16)
        zhc[p] = rcopy(zhsend.at[p], zhrecv.at[p], zh_s.at[p], zh_r.at[p], zh_dev)
        zhc[p].start()

    for a, out in ((0, mixed_ref), (1, gtok_ref)):
        sib[a, 0].wait_recv()
        total = own[a, 0] + sib_in[a, 0].astype(F32)
        for dx in (1, 3):
            arrived(xrecv.at[a, dx], tr_r.at[a, dx]).wait_recv()
            total = total + xrecv[a, dx].astype(F32)
        out[...] = total.astype(BF16)

    me = x * 2 + c
    ag = {}
    for p in PARTS:
        zhc[p].wait()
        fin[me, p] = (zhsend[p].astype(F32) + zhrecv[p].astype(F32)).astype(BF16)
        for dx in (2, 1, 3, 0):
            for dc in (1, 0):
                if dx or dc:
                    slot = ((4 - dx) % 4) * 2 + dc
                    ag[p, dx, dc] = rcopy(
                        fin.at[me, p], fin.at[me, p], ag_s.at[p, dx * 2 + dc], ag_r.at[p, slot], group(dx, dc)
                    )
                    ag[p, dx, dc].start()
    for p in PARTS:
        for dx in range(4):
            for dc in range(2):
                if dx or dc:
                    rank = ((x + dx) % 4) * 2 + (c if dc == 0 else sib_c)
                    arrived(fin.at[rank, p], ag_r.at[p, dx * 2 + dc]).wait_recv()

    def summed(t):
        p = 0 if t >= FIRST[0] else 1 if t < FIRST[2] else 2
        over = [n for n in range(4) if 0 <= t - FIRST[p] - start_of(p, n) < WIDE[p]][0]
        u = t - FIRST[p] - start_of(p, over)
        half = 0 if u < 2 else 1
        return fin[2 * over + half, p, u - core_start(p, half)]

    whole = load_gate_up(summed)
    ggate_ref[...] = whole[:, 0:HID]
    gup_ref[...] = whole[:, HID : 2 * HID]
    gdown_ref[...] = load_down(summed)

    @pl.when(remote)
    def _():
        for cp in wz:
            cp.wait_send()

    for key, cp in gz.items():
        if key[1]:
            cp.wait_send()
        else:

            @pl.when(jnp.logical_not(jnp.logical_and(keep, c == key[2])))
            def _(cp=cp):
                cp.wait_send()

    for cps in (tok, opp, fwd, wy, xy, sib, tro, tr, ag):
        for cp in cps.values():
            cp.wait_send()


def place(*refs):
    for i, o in zip(refs[:5], refs[5:]):
        o[...] = i[...]


def per_device(tokens, gate_weight, up_weight, down_weight, cotangent):
    dma = pltpu.SemaphoreType.DMA
    vm = pltpu.VMEM
    outs = (
        jax.ShapeDtypeStruct((D, ROWS), BF16),
        jax.ShapeDtypeStruct((D, ROWS), BF16),
        jax.ShapeDtypeStruct((DY, HID), BF16),
        jax.ShapeDtypeStruct((DY, HID), BF16),
        jax.ShapeDtypeStruct((DY, HID), BF16),
    )
    pieces = len(CUTS) - 1
    results = pl.pallas_call(
        kernel,
        out_shape=outs,
        in_specs=[pl.BlockSpec(memory_space=pl.ANY)] * 5,
        out_specs=[pl.BlockSpec(memory_space=vm)] * 5,
        scratch_shapes=[
            vm((2, 8, D, ROWS), BF16),
            vm((3, DY, HID), BF16),
            vm((TILES, 16, 128), BF16),
            vm((4, TILES, 16, 128), BF16),
            vm((D, 3 * HID), BF16),
            vm((HID, 8 * ROWS), F32),
            vm((HID, 8 * ROWS), F32),
            vm((2 * HID, 8 * ROWS), BF16),
            vm((HID, 8 * ROWS), BF16),
            vm((2, 4, D, ROWS), BF16),
            vm((2, 4, D, ROWS), F32),
            vm((2, 4, D, ROWS), BF16),
            vm((2, 4, D, ROWS), BF16),
            vm((2, 4, D, ROWS), BF16),
            vm((2, D, ROWS), BF16),
            vm((4, TILES, 16, 128), BF16),
            vm((4, 4, sum(WIDE), 16, 128), BF16),
            vm((3, 4, 2, 2, 16, 128), BF16),
            vm((3, 8, 2, 16, 128), BF16),
            vm((3, 2, 16, 128), BF16),
            vm((3, 2, 16, 128), BF16),
            vm((8, 3, 2, 16, 128), BF16),
            dma((5,)),
            dma((2, 4)), dma((2, 4)),
            dma((2, 7)), dma((2, 7)),
            dma((pieces,)), dma((pieces,)),
            dma((pieces, 4)), dma((pieces, 4)),
            dma((2, 4)), dma((2, 4)),
            dma((2, 4)), dma((2, 4)),
            dma((2, 4)), dma((2, 4)),
            dma((2, 4)), dma((2, 4)),
            dma((3, 4, 4)), dma((3, 4, 4)),
            dma((3, 4, 2)), dma((3, 8)),
            dma((3,)), dma((3,)),
            dma((3, 8)), dma((3, 8)),
            pltpu.SemaphoreType.REGULAR,
        ],
        compiler_params=pltpu.CompilerParams(
            collective_id=0, has_side_effects=True, vmem_limit_bytes=40 << 20
        ),
        name="swiglu",
    )(*[pltpu.with_memory_space_constraint(v, pltpu.HBM) for v in (tokens.T, gate_weight, up_weight, down_weight.T, cotangent.T)])
    mixed, gtok, ggate, gup, gdown = pl.pallas_call(
        place,
        out_shape=outs,
        in_specs=[pl.BlockSpec(memory_space=vm)] * 5,
        out_specs=[pl.BlockSpec(memory_space=vm)] * 5,
        compiler_params=pltpu.CompilerParams(vmem_limit_bytes=8 << 20),
        name="place",
    )(*results)
    return mixed.T, gtok.T, ggate, gup, gdown.T


def solution(mesh):
    return jax.shard_map(
        per_device,
        mesh=mesh,
        in_specs=(
            P(("dp", "fsdp", "tensor"), None),
            P("fsdp", "tensor"),
            P("fsdp", "tensor"),
            P("tensor", "fsdp"),
            P(("dp", "fsdp", "tensor"), None),
        ),
        out_specs=(
            P(("dp", "fsdp", "tensor"), None),
            P(("dp", "fsdp", "tensor"), None),
            P("fsdp", "tensor"),
            P("fsdp", "tensor"),
            P("tensor", "fsdp"),
        ),
        check_vma=False,
    )
```

```python
import jax
import jax.numpy as jnp
from jax import lax
from jax.experimental import pallas as pl
from jax.experimental.pallas import tpu as pltpu
from jax.sharding import PartitionSpec as P

MESH = pl.DeviceIdType.MESH
F32 = jnp.float32
BF16 = jnp.bfloat16

D = 576
ROWS = 128
DY = 144
HID = 192
TILES = 41
CUTS = (0, 7, 14, 21, 27, 34, 41)
GU_CUTS = 4
FIRST = (27, 0, 15)
WIDE = (4, 4, 3)
PLACE = (0, 4, 8)
PARTS = (0, 1, 2)


def start_of(part, x):
    return (4 * x - 2 * (x // 3), 4 * x - x // 3, 3 * x)[part]


def core_start(part, core):
    return (2 * core, 2 * core, core)[part]


def tn(left, right):
    return lax.dot_general(left, right, (((0,), (0,)), ((), ())), preferred_element_type=F32)


def nt(left, right):
    return lax.dot_general(left, right, (((1,), (1,)), ((), ())), preferred_element_type=F32)


def nn(left, right):
    return jnp.dot(left, right, preferred_element_type=F32)


def store_gate_up(ref, value):
    for r in range(9):
        for q in range(3):
            ref[3 * r + q] = value[16 * r : 16 * r + 16, 128 * q : 128 * q + 128]


def store_down(ref, value):
    for r in range(9):
        ref[27 + r] = value[16 * r : 16 * r + 16, 0:128]
    for i in range(4):
        ref[36 + i] = jnp.concatenate(
            [value[32 * i : 32 * i + 16, 128:192], value[32 * i + 16 : 32 * i + 32, 128:192]], axis=1
        )
    ref[40] = jnp.concatenate([value[128:144, 128:192], jnp.zeros((16, 64), value.dtype)], axis=1)


def load_gate_up(tile):
    return jnp.concatenate(
        [jnp.concatenate([tile(3 * r + q) for q in range(3)], axis=1) for r in range(9)], axis=0
    )


def load_down(tile):
    rows = []
    for r in range(9):
        last = tile(36 + r // 2)
        rows.append(jnp.concatenate([tile(27 + r), last[:, 0:64] if r % 2 == 0 else last[:, 64:128]], axis=1))
    return jnp.concatenate(rows, axis=0)


def kernel(
    tok_ref, gate_ref, up_ref, down_ref, cot_ref,
    mixed_ref, gtok_ref, ggate_ref, gup_ref, gdown_ref,
    xs, win, wmine, wrows, wall, swi, slo, ggu, hid, sib_out, own, sib_in, xsend, xrecv, xopp,
    ysend, xyr, zs, zr, zhsend, zhrecv, fin,
    in_s, tok_s, tok_r, fwd_s, fwd_r, wz_s, wz_r, wy_s, wy_r, opp_s, opp_r,
    sib_s, sib_r, tro_s, tro_r, tr_s, tr_r, xy_s, xy_r, gz_s, gz_r, zh_s, zh_r, ag_s, ag_r, far_sem,
):
    dp = lax.axis_index("dp")
    y = lax.axis_index("fsdp")
    zl = lax.axis_index("tensor")
    x, zh, c = dp // 4, (dp // 2) % 2, dp % 2
    z = zh * 8 + zl
    sib_c = 1 - c
    home = zl // 4

    def dev(xx, yy, zz, cc):
        zz = (zz + 16) % 16
        return (((xx + 4) % 4) * 4 + (zz // 8) * 2 + cc, (yy + 4) % 4, zz % 8)

    def group(dx, dc):
        return dev(x + dx, y, z, c if dc == 0 else sib_c)

    k_to = (c + home) % 2
    local = jnp.logical_and(x == 0, k_to == 0)
    remote = jnp.logical_not(local)
    zh_dev = dev(x, y, z + 8, c)

    def z_to(i):
        return dev(x, y, z + jnp.where(x == 0, 4 - 8 * (i % 2), 4 * k_to - x), home)


    shift = [jnp.where(((zl + r) % 4 + 4 * c - zl + 8) % 8 == r, r, r - 4) for r in range(4)]

    def rcopy(src, dst, ssem, rsem, to):
        return pltpu.make_async_remote_copy(
            src_ref=src, dst_ref=dst, send_sem=ssem, recv_sem=rsem, device_id=to, device_id_type=MESH
        )

    inputs = [
        pltpu.make_async_copy(gate_ref, win.at[0], in_s.at[0]),
        pltpu.make_async_copy(up_ref, win.at[1], in_s.at[0]),
        pltpu.make_async_copy(down_ref, win.at[2], in_s.at[0]),
        pltpu.make_async_copy(tok_ref, xs.at[0, 0], in_s.at[1]),
        pltpu.make_async_copy(cot_ref, xs.at[1, 0], in_s.at[1]),
    ]
    for cp in inputs:
        cp.start()

    def arrived(ref, sem):
        rcopy(ref, ref, sem, sem, group(0, 1)).wait_recv()

    def sent(ref, sem):
        rcopy(ref, ref, sem, sem, group(0, 1)).wait_send()

    barrier = pltpu.get_barrier_semaphore()

    def greet(to):
        pl.semaphore_signal(barrier, inc=1, device_id=to, device_id_type=MESH)

    for s in (4, -4):
        for h in range(2):
            greet(dev(x, y, z + s, h))
    for s in (3, -3, 2, -2, 1, -1):
        greet(dev(x, y, z - s, home))
    for r in (3, 2, 1):
        for h in range(2):
            greet(dev(x, y, z + shift[r], h))
    for dx in (2, 1, 3, 0):
        for d in (2, 1, 3, 0):
            if dx or d:
                greet(dev(x + dx, y + d, z, c))
        greet(group(dx, 1))

    pltpu.make_async_copy(win, win, in_s.at[0]).wait()
    store_gate_up(wmine, jnp.concatenate([win[0], win[1]], axis=1))
    store_down(wmine, win[2])
    pltpu.make_async_copy(xs.at[0, pl.ds(0, 2)], xs.at[0, pl.ds(0, 2)], in_s.at[1]).wait()

    pl.semaphore_wait(barrier, 35)

    pl.semaphore_signal(far_sem, inc=1, device_id=dev(x, y, z - 4, c), device_id_type=MESH)

    def cut(ref, i):
        return ref.at[pl.ds(CUTS[i], CUTS[i + 1] - CUTS[i])]

    wz = [
        rcopy(cut(wmine, i), cut(wrows.at[0], i), wz_s, wz_r.at[i], z_to(i)) for i in range(len(CUTS) - 1)
    ]

    @pl.when(remote)
    def _():
        for cp in wz:
            cp.start()

    halves = {1: pl.ds(0, D // 2), 3: pl.ds(D // 2, D // 2)}
    for a in (0, 1):
        for dx in (1, 3):
            rcopy(xs.at[a, 0], xs.at[a, 2 * (4 - dx)], tok_s, tok_r.at[a], group(dx, 0)).start()
    for a in (0, 1):
        rcopy(xs.at[a, 0], xs.at[a, 1], fwd_s, fwd_r.at[a, 0], group(0, 1)).start()

    @pl.when(local)
    def _():
        wrows[0] = wmine[...]

    def pass_on(a):
        arrived(xs.at[a, pl.ds(2, 2)], tok_r.at[a])
        for dx in (1, 3):
            rcopy(
                xs.at[a, 2 * dx, halves[dx]], xs.at[a, 4, halves[dx]], opp_s, opp_r.at[a], group(4 - dx, 0)
            ).start()
            rcopy(xs.at[a, 2 * dx], xs.at[a, 2 * dx + 1], fwd_s, fwd_r.at[a, 1], group(0, 1)).start()

    def pass_on_opposite(a):
        arrived(xs.at[a, 4], opp_r.at[a])
        rcopy(xs.at[a, 4], xs.at[a, 5], fwd_s, fwd_r.at[a, 2], group(0, 1)).start()

    def wait_pair(a, dx):
        if dx != 3:
            arrived(xs.at[a, pl.ds(2, 2)] if dx == 1 else xs.at[a, 5], fwd_r.at[a, dx])

    for i in range(len(CUTS) - 1):

        @pl.when(remote)
        def _(i=i):
            arrived(cut(wrows.at[0], i), wz_r.at[i])

        for d in (2, 1, 3):
            rcopy(
                cut(wrows.at[0], i), cut(wrows.at[4 - d], i), wy_s, wy_r.at[i], dev(x, y + d, z, c)
            ).start()
        if i == 1:
            pass_on(0)
        if i == 4:
            pass_on(1)

    def from_y(i):
        arrived(wrows.at[pl.ds(1, 3), pl.ds(CUTS[i], CUTS[i + 1] - CUTS[i])], wy_r.at[i])

    def pair(a, dx):
        return jnp.concatenate([xs[a, 2 * dx], xs[a, 2 * dx + 1]], axis=1)

    pass_on_opposite(0)
    for i in range(GU_CUTS):
        from_y(i)
    for d in range(4):
        rows = pl.ds(pl.multiple_of(((y + d) % 4) * DY, 16), DY)
        wall[rows, 0 : 2 * HID] = load_gate_up(lambda t: wrows[d, t])
    for dx in (0, 1, 3, 2):
        if dx == 2:
            pass_on_opposite(1)
        cols = pl.ds(dx * 256, 256)
        wait_pair(0, dx)
        sums = tn(wall[:, 0 : 2 * HID], pair(0, dx))
        gate_sum, up_sum = sums[0:HID], sums[HID : 2 * HID]
        sig = jax.nn.sigmoid(gate_sum)
        swished = gate_sum * sig
        swi[:, cols] = swished
        slo[:, cols] = up_sum * sig * (1.0 + gate_sum * (1.0 - sig))
        hid[:, cols] = (swished * up_sum).astype(BF16)
    for dx in (0, 1, 3, 2):
        wait_pair(1, dx)

    def spread(p, d):
        for dx in (2, 1, 3, 0):
            piece = ysend.at[(y + d) % 4, pl.ds(FIRST[p] + start_of(p, (x + dx) % 4), WIDE[p])]
            there = ((4 - dx) % 4) * 4 + (4 - d) % 4
            place = pl.ds(PLACE[p], WIDE[p])
            if d or dx:
                rcopy(piece, xyr.at[there, place], xy_s, xy_r.at[p], dev(x + dx, y + d, z, c)).start()
            else:
                xyr[0, place] = piece[...]

    def all_of(a):
        return jnp.concatenate([xs[a, s] for s in range(8)], axis=1)

    down_grad = nt(all_of(1), hid[...]).astype(BF16)
    for n in range(4):
        store_down(ysend.at[n], down_grad[DY * n : DY * n + DY])
    for d in (2, 1, 3, 0):
        spread(0, d)
    for i in range(GU_CUTS, len(CUTS) - 1):
        from_y(i)
    for d in range(4):
        rows = pl.ds(pl.multiple_of(((y + d) % 4) * DY, 16), DY)
        wall[rows, 2 * HID : 3 * HID] = load_down(lambda t: wrows[d, t])
    for dx in (0, 1, 3, 2):
        cols = pl.ds(dx * 256, 256)
        grad_hidden = tn(wall[:, 2 * HID : 3 * HID], pair(1, dx))
        ggu[0:HID, cols] = (grad_hidden * slo[:, cols]).astype(BF16)
        ggu[HID : 2 * HID, cols] = (grad_hidden * swi[:, cols]).astype(BF16)
    gate_up_grad = nt(all_of(0), ggu[...]).astype(BF16)
    for n in range(4):
        store_gate_up(ysend.at[n], gate_up_grad[DY * n : DY * n + DY])
    for p in (1, 2):
        for d in (2, 1, 3, 0):
            spread(p, d)

    for dx in (2, 1, 3, 0):
        cols = pl.ds(dx * 256, 256)
        for a in (0, 1):
            part = nn(wall[:, 2 * HID : 3 * HID], hid[:, cols]) if a == 0 else nn(wall[:, 0 : 2 * HID], ggu[:, cols])
            own[a, dx] = part[:, 0:ROWS]
            sib_out[dx, a] = part[:, ROWS : 2 * ROWS].astype(BF16)
            rcopy(
                sib_out.at[dx, a], sib_in.at[dx, a], sib_s, sib_r.at[0 if dx == 2 else 1], group(0, 1)
            ).start()
    arrived(sib_in.at[2], sib_r.at[0])
    for a in (0, 1):
        xsend[a, 2] = (own[a, 2] + sib_in[2, a].astype(F32)).astype(BF16)
        for dx in (1, 3):
            rcopy(xsend.at[a, 2, halves[dx]], xopp.at[a, halves[dx]], tro_s, tro_r, group(dx, 0)).start()

    keep = c == home
    for p in PARTS:
        arrived(xyr.at[pl.ds(1, 15), pl.ds(PLACE[p], WIDE[p])], xy_r.at[p])
        for r in (0, 3, 1, 2):
            there = ((r - x + 4) % 4) * 4
            total = xyr[there, PLACE[p] : PLACE[p] + WIDE[p]].astype(F32)
            for d in (1, 2, 3):
                total = total + xyr[there + d, PLACE[p] : PLACE[p] + WIDE[p]].astype(F32)
            total = total.astype(BF16)
            slot = (shift[r] + 8) % 8
            for h in range(2):
                zs[p, r, h] = total[core_start(p, h) : core_start(p, h) + 2]
                far = jnp.where(shift[r] == -4, 4 - 8 * h, shift[r])
                step = rcopy(zs.at[p, r, h], zr.at[p, slot], gz_s, gz_r.at[p], dev(x, y, z + far, h))
                if r:
                    step.start()
                else:
                    stays = jnp.logical_and(keep, c == h)

                    @pl.when(jnp.logical_not(stays))
                    def _(step=step):
                        step.start()

                    @pl.when(stays)
                    def _(p=p, h=h):
                        zr[p, 0] = zs[p, 0, h]

    arrived(sib_in.at[pl.ds(0, 3)], sib_r.at[1])
    arrived(xopp, tro_r)
    for a in (0, 1):
        for dx in (1, 3):
            part = own[a, dx] + sib_in[dx, a].astype(F32)
            extra = xopp[a, halves[dx]].astype(F32)
            if dx == 1:
                part = jnp.concatenate([part[0 : D // 2] + extra, part[D // 2 : D]], axis=0)
            else:
                part = jnp.concatenate([part[0 : D // 2], part[D // 2 : D] + extra], axis=0)
            xsend[a, dx] = part.astype(BF16)
            rcopy(xsend.at[a, dx], xrecv.at[a, (4 - dx) // 2], tr_s, tr_r.at[a], group(dx, 0)).start()

    pl.semaphore_wait(far_sem, 1)
    for p in PARTS:

        @pl.when(keep)
        def _(p=p):
            arrived(zr.at[p, pl.ds(1, 7)], gz_r.at[p])

        @pl.when(jnp.logical_not(keep))
        def _(p=p):
            arrived(zr.at[p], gz_r.at[p])

        total = zr[p, 0].astype(F32)
        for s in range(1, 8):
            total = total + zr[p, s].astype(F32)
        zhsend[p] = total.astype(BF16)
        rcopy(zhsend.at[p], zhrecv.at[p], zh_s, zh_r.at[p], zh_dev).start()

    for a, out in ((0, mixed_ref), (1, gtok_ref)):
        arrived(xrecv.at[a], tr_r.at[a])
        total = own[a, 0] + sib_in[0, a].astype(F32)
        for n in range(2):
            total = total + xrecv[a, n].astype(F32)
        out[...] = total.astype(BF16)

    me = x * 2 + c
    for p in PARTS:
        arrived(zhrecv.at[p], zh_r.at[p])
        fin[me, p] = (zhsend[p].astype(F32) + zhrecv[p].astype(F32)).astype(BF16)
        for dx in (2, 1, 3, 0):
            for dc in (1, 0):
                if dx or dc:
                    rcopy(fin.at[me, p], fin.at[me, p], ag_s, ag_r.at[p], group(dx, dc)).start()
    for p in PARTS:
        arrived(fin.at[pl.ds(0, 7), p], ag_r.at[p])

    def summed(t):
        p = 0 if t >= FIRST[0] else 1 if t < FIRST[2] else 2
        over = [n for n in range(4) if 0 <= t - FIRST[p] - start_of(p, n) < WIDE[p]][0]
        u = t - FIRST[p] - start_of(p, over)
        half = 0 if u < 2 else 1
        return fin[2 * over + half, p, u - core_start(p, half)]

    whole = load_gate_up(summed)
    ggate_ref[...] = whole[:, 0:HID]
    gup_ref[...] = whole[:, HID : 2 * HID]
    gdown_ref[...] = load_down(summed)

    @pl.when(remote)
    def _():
        sent(wmine, wz_s)

    @pl.when(keep)
    def _():
        sent(zr.at[pl.ds(0, 3), pl.ds(1, 7)], gz_s)

    @pl.when(jnp.logical_not(keep))
    def _():
        sent(zr, gz_s)

    sent(xs.at[0, pl.ds(0, 4)], tok_s)
    sent(xs.at[0, pl.ds(0, 2)], opp_s)
    sent(xs.at[0], fwd_s)
    sent(wrows.at[pl.ds(1, 3)], wy_s)
    sent(xyr.at[pl.ds(1, 15)], xy_s)
    sent(sib_out, sib_s)
    sent(xopp, tro_s)
    sent(xrecv, tr_s)
    sent(zhsend, zh_s)
    sent(fin.at[pl.ds(0, 7)], ag_s)


def place(*refs):
    for i, o in zip(refs[:5], refs[5:]):
        o[...] = i[...]


def per_device(tokens, gate_weight, up_weight, down_weight, cotangent):
    dma = pltpu.SemaphoreType.DMA
    vm = pltpu.VMEM
    outs = (
        jax.ShapeDtypeStruct((D, ROWS), BF16),
        jax.ShapeDtypeStruct((D, ROWS), BF16),
        jax.ShapeDtypeStruct((DY, HID), BF16),
        jax.ShapeDtypeStruct((DY, HID), BF16),
        jax.ShapeDtypeStruct((DY, HID), BF16),
    )
    pieces = len(CUTS) - 1
    results = pl.pallas_call(
        kernel,
        out_shape=outs,
        in_specs=[pl.BlockSpec(memory_space=pl.ANY)] * 5,
        out_specs=[pl.BlockSpec(memory_space=vm)] * 5,
        scratch_shapes=[
            vm((2, 8, D, ROWS), BF16),
            vm((3, DY, HID), BF16),
            vm((TILES, 16, 128), BF16),
            vm((4, TILES, 16, 128), BF16),
            vm((D, 3 * HID), BF16),
            vm((HID, 8 * ROWS), F32),
            vm((HID, 8 * ROWS), F32),
            vm((2 * HID, 8 * ROWS), BF16),
            vm((HID, 8 * ROWS), BF16),
            vm((4, 2, D, ROWS), BF16),
            vm((2, 4, D, ROWS), F32),
            vm((4, 2, D, ROWS), BF16),
            vm((2, 4, D, ROWS), BF16),
            vm((2, 2, D, ROWS), BF16),
            vm((2, D, ROWS), BF16),
            vm((4, TILES, 16, 128), BF16),
            vm((16, sum(WIDE), 16, 128), BF16),
            vm((3, 4, 2, 2, 16, 128), BF16),
            vm((3, 8, 2, 16, 128), BF16),
            vm((3, 2, 16, 128), BF16),
            vm((3, 2, 16, 128), BF16),
            vm((8, 3, 2, 16, 128), BF16),
            dma((2,)),
            dma, dma((2,)),
            dma, dma((2, 3)),
            dma, dma((pieces,)),
            dma, dma((pieces,)),
            dma, dma((2,)),
            dma, dma((2,)),
            dma, dma,
            dma, dma((2,)),
            dma, dma((3,)),
            dma, dma((3,)),
            dma, dma((3,)),
            dma, dma((3,)),
            pltpu.SemaphoreType.REGULAR,
        ],
        compiler_params=pltpu.CompilerParams(
            collective_id=0, has_side_effects=True, vmem_limit_bytes=40 << 20
        ),
        name="swiglu",
    )(*[pltpu.with_memory_space_constraint(v, pltpu.HBM) for v in (tokens.T, gate_weight, up_weight, down_weight.T, cotangent.T)])
    mixed, gtok, ggate, gup, gdown = pl.pallas_call(
        place,
        out_shape=outs,
        in_specs=[pl.BlockSpec(memory_space=vm)] * 5,
        out_specs=[pl.BlockSpec(memory_space=vm)] * 5,
        compiler_params=pltpu.CompilerParams(vmem_limit_bytes=8 << 20),
        name="place",
    )(*results)
    return mixed.T, gtok.T, ggate, gup, gdown.T


def solution(mesh):
    return jax.shard_map(
        per_device,
        mesh=mesh,
        in_specs=(
            P(("dp", "fsdp", "tensor"), None),
            P("fsdp", "tensor"),
            P("fsdp", "tensor"),
            P("tensor", "fsdp"),
            P(("dp", "fsdp", "tensor"), None),
        ),
        out_specs=(
            P(("dp", "fsdp", "tensor"), None),
            P(("dp", "fsdp", "tensor"), None),
            P("fsdp", "tensor"),
            P("fsdp", "tensor"),
            P("tensor", "fsdp"),
        ),
        check_vma=False,
    )
```

```python
import jax
import jax.numpy as jnp
from jax import lax
from jax.experimental import pallas as pl
from jax.experimental.pallas import tpu as pltpu
from jax.sharding import PartitionSpec as P

MESH = pl.DeviceIdType.MESH
F32 = jnp.float32
BF16 = jnp.bfloat16

D = 576
ROWS = 128
DY = 144
HID = 192
TILES = 41
CUTS = (0, 7, 14, 21, 27, 34, 41)
GU_CUTS = 4
FIRST = (27, 0, 15)
WIDE = (4, 4, 3)
PLACE = (0, 4, 8)
PARTS = (0, 1, 2)


def start_of(part, x):
    return (4 * x - 2 * (x // 3), 4 * x - x // 3, 3 * x)[part]


def core_start(part, core):
    return (2 * core, 2 * core, core)[part]


def tn(left, right):
    return lax.dot_general(left, right, (((0,), (0,)), ((), ())), preferred_element_type=F32)


def nt(left, right):
    return lax.dot_general(left, right, (((1,), (1,)), ((), ())), preferred_element_type=F32)


def nn(left, right):
    return jnp.dot(left, right, preferred_element_type=F32)


def store_gate_up(ref, value):
    for r in range(9):
        for q in range(3):
            ref[3 * r + q] = value[16 * r : 16 * r + 16, 128 * q : 128 * q + 128]


def store_down(ref, value):
    for r in range(9):
        ref[27 + r] = value[16 * r : 16 * r + 16, 0:128]
    for i in range(4):
        ref[36 + i] = jnp.concatenate(
            [value[32 * i : 32 * i + 16, 128:192], value[32 * i + 16 : 32 * i + 32, 128:192]], axis=1
        )
    ref[40] = jnp.concatenate([value[128:144, 128:192], jnp.zeros((16, 64), value.dtype)], axis=1)


def load_gate_up(tile):
    return jnp.concatenate(
        [jnp.concatenate([tile(3 * r + q) for q in range(3)], axis=1) for r in range(9)], axis=0
    )


def load_down(tile):
    rows = []
    for r in range(9):
        last = tile(36 + r // 2)
        rows.append(jnp.concatenate([tile(27 + r), last[:, 0:64] if r % 2 == 0 else last[:, 64:128]], axis=1))
    return jnp.concatenate(rows, axis=0)


def kernel(
    tok_ref, gate_ref, up_ref, down_ref, cot_ref,
    mixed_ref, gtok_ref, ggate_ref, gup_ref, gdown_ref,
    xs, win, wmine, wrows, wall, swi, slo, ggu, hid, sib_out, own, sib_in, xsend, xrecv, xopp,
    ysend, down_early, xyr, zs, zr, zhsend, zhrecv, fin,
    in_s, tok_s, tok_r, fwd_s, fwd_r, wz_s, wz_r, wy_s, wy_r, opp_s, opp_r,
    sib_s, sib_r, tro_s, tro_r, tr_s, tr_r, xy_s, xy_r, gz_s, gz_r, zh_s, zh_r, ag_s, ag_r,
):
    dp = lax.axis_index("dp")
    y = lax.axis_index("fsdp")
    zl = lax.axis_index("tensor")
    x, zh, c = dp // 4, (dp // 2) % 2, dp % 2
    z = zh * 8 + zl
    sib_c = 1 - c
    home = zl // 4

    def dev(xx, yy, zz, cc):
        zz = (zz + 16) % 16
        return (((xx + 4) % 4) * 4 + (zz // 8) * 2 + cc, (yy + 4) % 4, zz % 8)

    def group(dx, dc):
        return dev(x + dx, y, z, c if dc == 0 else sib_c)

    k_to = (c + home) % 2
    local = jnp.logical_and(x == 0, k_to == 0)
    remote = jnp.logical_not(local)

    def z_to(i):
        return dev(x, y, z + jnp.where(x == 0, 4 - 8 * (i % 2), 4 * k_to - x), home)


    shift = [jnp.where(((zl + r) % 4 + 4 * c - zl + 8) % 8 == r, r - 4, r) for r in range(4)]

    def rcopy(src, dst, ssem, rsem, to):
        return pltpu.make_async_remote_copy(
            src_ref=src, dst_ref=dst, send_sem=ssem, recv_sem=rsem, device_id=to, device_id_type=MESH
        )

    inputs = [
        pltpu.make_async_copy(gate_ref, win.at[0], in_s.at[0]),
        pltpu.make_async_copy(up_ref, win.at[1], in_s.at[0]),
        pltpu.make_async_copy(down_ref, win.at[2], in_s.at[0]),
        pltpu.make_async_copy(tok_ref, xs.at[0, 0], in_s.at[1]),
        pltpu.make_async_copy(cot_ref, xs.at[1, 0], in_s.at[1]),
    ]
    for cp in inputs:
        cp.start()

    def arrived(ref, sem):
        rcopy(ref, ref, sem, sem, group(0, 1)).wait_recv()

    def sent(ref, sem):
        rcopy(ref, ref, sem, sem, group(0, 1)).wait_send()

    barrier = pltpu.get_barrier_semaphore()

    def greet(to):
        pl.semaphore_signal(barrier, inc=1, device_id=to, device_id_type=MESH)

    for dx in (1, 3):
        greet(group(dx, 0))
    for s in (4, -4, 3, -3, 2, -2, 1, -1):
        for h in range(2):
            greet(dev(x, y, z + s, h))
    for dx in (2, 1, 3, 0):
        for d in (2, 1, 3, 0):
            if d or dx == 2:
                greet(dev(x + dx, y + d, z, c))
        greet(group(dx, 1))

    pltpu.make_async_copy(xs.at[0, pl.ds(0, 2)], xs.at[0, pl.ds(0, 2)], in_s.at[1]).wait()
    pl.semaphore_wait(barrier, 35)

    halves = {1: pl.ds(0, D // 2), 3: pl.ds(D // 2, D // 2)}
    for a in (0, 1):
        for late in (0, 1):
            for dx in (1, 3):
                rows = halves[dx if late else 4 - dx]
                rcopy(
                    xs.at[a, 0, rows], xs.at[a, 2 * (4 - dx), rows], tok_s, tok_r.at[a, late], group(dx, 0)
                ).start()

    pltpu.make_async_copy(win, win, in_s.at[0]).wait()
    store_gate_up(wmine, jnp.concatenate([win[0], win[1]], axis=1))
    store_down(wmine, win[2])

    def cut(ref, i):
        return ref.at[pl.ds(CUTS[i], CUTS[i + 1] - CUTS[i])]

    wz = [
        rcopy(cut(wmine, i), cut(wrows.at[0], i), wz_s, wz_r.at[i], z_to(i)) for i in range(len(CUTS) - 1)
    ]

    @pl.when(remote)
    def _():
        for cp in wz:
            cp.start()

    for a in (0, 1):
        rcopy(xs.at[a, 0], xs.at[a, 1], fwd_s, fwd_r.at[a, 0], group(0, 1)).start()

    @pl.when(local)
    def _():
        wrows[0] = wmine[...]

    def pass_on(a, late):
        arrived(xs.at[a, 2], tok_r.at[a, late])
        for dx in (1, 3):
            rows = halves[4 - dx if late else dx]
            if not late:
                rcopy(xs.at[a, 2 * dx, rows], xs.at[a, 4, rows], opp_s, opp_r.at[a], group(4 - dx, 0)).start()
            rcopy(xs.at[a, 2 * dx, rows], xs.at[a, 2 * dx + 1, rows], fwd_s, fwd_r.at[a, 1], group(0, 1)).start()

    def pass_on_opposite(a):
        arrived(xs.at[a, 4], opp_r.at[a])
        rcopy(xs.at[a, 4], xs.at[a, 5], fwd_s, fwd_r.at[a, 2], group(0, 1)).start()

    def wait_pair(a, dx):
        if dx != 3:
            arrived(xs.at[a, pl.ds(2, 2)] if dx == 1 else xs.at[a, 5], fwd_r.at[a, dx])

    for i in range(len(CUTS) - 1):

        @pl.when(remote)
        def _(i=i):
            arrived(cut(wrows.at[0], i), wz_r.at[i])

        for d in (2, 1, 3):
            rcopy(
                cut(wrows.at[0], i), cut(wrows.at[4 - d], i), wy_s, wy_r.at[i], dev(x, y + d, z, c)
            ).start()
        if i in (0, 2, 4, 5):
            pass_on(int(i > 2), int(i in (2, 5)))

    def from_y(i):
        arrived(wrows.at[pl.ds(1, 3), pl.ds(CUTS[i], CUTS[i + 1] - CUTS[i])], wy_r.at[i])

    def pair(a, dx):
        return jnp.concatenate([xs[a, 2 * dx], xs[a, 2 * dx + 1]], axis=1)

    pass_on_opposite(0)
    for i in range(GU_CUTS):
        from_y(i)
    for d in range(4):
        rows = pl.ds(pl.multiple_of(((y + d) % 4) * DY, 16), DY)
        wall[rows, 0 : 2 * HID] = load_gate_up(lambda t: wrows[d, t])
    for dx in (0, 1, 3, 2):
        if dx == 2:
            pass_on_opposite(1)
        cols = pl.ds(dx * 256, 256)
        wait_pair(0, dx)
        sums = tn(wall[:, 0 : 2 * HID], pair(0, dx))
        gate_sum, up_sum = sums[0:HID], sums[HID : 2 * HID]
        sig = jax.nn.sigmoid(gate_sum)
        swished = gate_sum * sig
        swi[:, cols] = swished
        slo[:, cols] = up_sum * sig * (1.0 + gate_sum * (1.0 - sig))
        hid[:, cols] = (swished * up_sum).astype(BF16)
    for dx in (0, 1, 3):
        wait_pair(1, dx)
    early = jnp.concatenate([xs[1, n] for n in (0, 1, 2, 3, 6, 7)], axis=1)
    down_early[...] = nt(early, jnp.concatenate([hid[:, 0:512], hid[:, 768:1024]], axis=1))
    wait_pair(1, 2)

    def spread(p, d):
        for dx in (2, 1, 3, 0):
            piece = ysend.at[(y + d) % 4, pl.ds(FIRST[p] + start_of(p, (x + dx) % 4), WIDE[p])]
            there = ((4 - dx) % 4) * 4 + (4 - d) % 4
            place = pl.ds(PLACE[p], WIDE[p])
            if d or dx:
                rcopy(piece, xyr.at[there, place], xy_s, xy_r.at[p], dev(x + dx, y + d, z, c)).start()
            else:
                xyr[0, place] = piece[...]

    down_grad = (down_early[...] + nt(pair(1, 2), hid[:, 512:768])).astype(BF16)
    for n in range(4):
        store_down(ysend.at[n], down_grad[DY * n : DY * n + DY])
    for d in (2, 1, 3, 0):
        spread(0, d)
    for i in range(GU_CUTS, len(CUTS) - 1):
        from_y(i)
    for d in range(4):
        rows = pl.ds(pl.multiple_of(((y + d) % 4) * DY, 16), DY)
        wall[rows, 2 * HID : 3 * HID] = load_down(lambda t: wrows[d, t])
    for dx in (0, 1, 3, 2):
        cols = pl.ds(dx * 256, 256)
        grad_hidden = tn(wall[:, 2 * HID : 3 * HID], pair(1, dx))
        ggu[0:HID, cols] = (grad_hidden * slo[:, cols]).astype(BF16)
        ggu[HID : 2 * HID, cols] = (grad_hidden * swi[:, cols]).astype(BF16)
    gate_up_grad = nt(jnp.concatenate([xs[0, n] for n in range(8)], axis=1), ggu[...]).astype(BF16)
    for n in range(4):
        store_gate_up(ysend.at[n], gate_up_grad[DY * n : DY * n + DY])
    for p in (1, 2):
        for d in (2, 1, 3, 0):
            spread(p, d)

    for dx in (2, 1, 3, 0):
        cols = pl.ds(dx * 256, 256)
        for a in (0, 1):
            part = nn(wall[:, 2 * HID : 3 * HID], hid[:, cols]) if a == 0 else nn(wall[:, 0 : 2 * HID], ggu[:, cols])
            own[a, dx] = part[:, 0:ROWS]
            sib_out[dx, a] = part[:, ROWS : 2 * ROWS].astype(BF16)
            rcopy(
                sib_out.at[dx, a], sib_in.at[dx, a], sib_s, sib_r.at[0 if dx == 2 else 1], group(0, 1)
            ).start()
    arrived(sib_in.at[2], sib_r.at[0])
    for a in (0, 1):
        xsend[a, 2] = (own[a, 2] + sib_in[2, a].astype(F32)).astype(BF16)
        for dx in (1, 3):
            rcopy(xsend.at[a, 2, halves[dx]], xopp.at[a, halves[dx]], tro_s, tro_r, group(dx, 0)).start()

    keep = c != home
    for p in PARTS:
        arrived(xyr.at[pl.ds(1, 15), pl.ds(PLACE[p], WIDE[p])], xy_r.at[p])
        for r in (0, 3, 1, 2):
            there = ((r - x + 4) % 4) * 4
            total = xyr[there, PLACE[p] : PLACE[p] + WIDE[p]].astype(F32)
            for d in (1, 2, 3):
                total = total + xyr[there + d, PLACE[p] : PLACE[p] + WIDE[p]].astype(F32)
            total = total.astype(BF16)
            slot = (shift[r] + 8) % 8
            for h in range(2):
                zs[p, r, h] = total[core_start(p, h) : core_start(p, h) + 2]
                far = jnp.where(shift[r] == -4, 4 - 8 * h, shift[r])
                step = rcopy(zs.at[p, r, h], zr.at[p, slot], gz_s, gz_r.at[p], dev(x, y, z + far, h))
                if r:
                    step.start()
                else:
                    stays = jnp.logical_and(keep, c == h)

                    @pl.when(jnp.logical_not(stays))
                    def _(step=step):
                        step.start()

                    @pl.when(stays)
                    def _(p=p, h=h):
                        zr[p, 0] = zs[p, 0, h]

    arrived(sib_in.at[pl.ds(0, 3)], sib_r.at[1])
    arrived(xopp, tro_r)
    for a in (0, 1):
        for dx in (1, 3):
            part = own[a, dx] + sib_in[dx, a].astype(F32)
            extra = xopp[a, halves[dx]].astype(F32)
            if dx == 1:
                part = jnp.concatenate([part[0 : D // 2] + extra, part[D // 2 : D]], axis=0)
            else:
                part = jnp.concatenate([part[0 : D // 2], part[D // 2 : D] + extra], axis=0)
            xsend[a, dx] = part.astype(BF16)
            rcopy(xsend.at[a, dx], xrecv.at[a, (4 - dx) // 2], tr_s, tr_r.at[a], group(dx, 0)).start()

    for p in PARTS:

        @pl.when(keep)
        def _(p=p):
            arrived(zr.at[p, pl.ds(1, 7)], gz_r.at[p])

        @pl.when(jnp.logical_not(keep))
        def _(p=p):
            arrived(zr.at[p], gz_r.at[p])

        total = zr[p, 0].astype(F32)
        for s in range(1, 8):
            total = total + zr[p, s].astype(F32)
        zhsend[p] = total.astype(BF16)
        for n in range(2):
            rcopy(zhsend.at[p], zhrecv.at[p, n], zh_s, zh_r.at[p], dev(x, y, z + 4 - 8 * n, c)).start()

    me = x * 2 + c
    for p in PARTS:
        arrived(zhrecv.at[p], zh_r.at[p])
        fin[me, p] = (zhrecv[p, 0].astype(F32) + zhrecv[p, 1].astype(F32)).astype(BF16)
        for dx in (2, 1, 3, 0):
            for dc in (1, 0):
                if dx or dc:
                    rcopy(fin.at[me, p], fin.at[me, p], ag_s, ag_r.at[p], group(dx, dc)).start()
    for a, out in ((0, mixed_ref), (1, gtok_ref)):
        arrived(xrecv.at[a], tr_r.at[a])
        total = own[a, 0] + sib_in[0, a].astype(F32)
        for n in range(2):
            total = total + xrecv[a, n].astype(F32)
        out[...] = total.astype(BF16)

    for p in PARTS:
        arrived(fin.at[pl.ds(0, 7), p], ag_r.at[p])

    def summed(t):
        p = 0 if t >= FIRST[0] else 1 if t < FIRST[2] else 2
        over = [n for n in range(4) if 0 <= t - FIRST[p] - start_of(p, n) < WIDE[p]][0]
        u = t - FIRST[p] - start_of(p, over)
        half = 0 if u < 2 else 1
        return fin[2 * over + half, p, u - core_start(p, half)]

    whole = load_gate_up(summed)
    ggate_ref[...] = whole[:, 0:HID]
    gup_ref[...] = whole[:, HID : 2 * HID]
    gdown_ref[...] = load_down(summed)

    @pl.when(remote)
    def _():
        sent(wmine, wz_s)

    @pl.when(keep)
    def _():
        sent(zr.at[pl.ds(0, 3), pl.ds(1, 7)], gz_s)

    @pl.when(jnp.logical_not(keep))
    def _():
        sent(zr, gz_s)

    sent(xs.at[0, pl.ds(0, 4)], tok_s)
    sent(xs.at[0, pl.ds(0, 2)], opp_s)
    sent(xs.at[0], fwd_s)
    sent(wrows.at[pl.ds(1, 3)], wy_s)
    sent(xyr.at[pl.ds(1, 15)], xy_s)
    sent(sib_out, sib_s)
    sent(xopp, tro_s)
    sent(xrecv, tr_s)
    sent(zhrecv, zh_s)
    sent(fin.at[pl.ds(0, 7)], ag_s)


def place(*refs):
    for i, o in zip(refs[:5], refs[5:]):
        o[...] = i[...]


def per_device(tokens, gate_weight, up_weight, down_weight, cotangent):
    dma = pltpu.SemaphoreType.DMA
    vm = pltpu.VMEM
    outs = (
        jax.ShapeDtypeStruct((D, ROWS), BF16),
        jax.ShapeDtypeStruct((D, ROWS), BF16),
        jax.ShapeDtypeStruct((DY, HID), BF16),
        jax.ShapeDtypeStruct((DY, HID), BF16),
        jax.ShapeDtypeStruct((DY, HID), BF16),
    )
    pieces = len(CUTS) - 1
    results = pl.pallas_call(
        kernel,
        out_shape=outs,
        in_specs=[pl.BlockSpec(memory_space=pl.ANY)] * 5,
        out_specs=[pl.BlockSpec(memory_space=vm)] * 5,
        scratch_shapes=[
            vm((2, 8, D, ROWS), BF16),
            vm((3, DY, HID), BF16),
            vm((TILES, 16, 128), BF16),
            vm((4, TILES, 16, 128), BF16),
            vm((D, 3 * HID), BF16),
            vm((HID, 8 * ROWS), F32),
            vm((HID, 8 * ROWS), F32),
            vm((2 * HID, 8 * ROWS), BF16),
            vm((HID, 8 * ROWS), BF16),
            vm((4, 2, D, ROWS), BF16),
            vm((2, 4, D, ROWS), F32),
            vm((4, 2, D, ROWS), BF16),
            vm((2, 4, D, ROWS), BF16),
            vm((2, 2, D, ROWS), BF16),
            vm((2, D, ROWS), BF16),
            vm((4, TILES, 16, 128), BF16),
            vm((D, HID), F32),
            vm((16, sum(WIDE), 16, 128), BF16),
            vm((3, 4, 2, 2, 16, 128), BF16),
            vm((3, 8, 2, 16, 128), BF16),
            vm((3, 2, 16, 128), BF16),
            vm((3, 2, 2, 16, 128), BF16),
            vm((8, 3, 2, 16, 128), BF16),
            dma((2,)),
            dma, dma((2, 2)),
            dma, dma((2, 3)),
            dma, dma((pieces,)),
            dma, dma((pieces,)),
            dma, dma((2,)),
            dma, dma((2,)),
            dma, dma,
            dma, dma((2,)),
            dma, dma((3,)),
            dma, dma((3,)),
            dma, dma((3,)),
            dma, dma((3,)),
        ],
        compiler_params=pltpu.CompilerParams(
            collective_id=0, has_side_effects=True, vmem_limit_bytes=40 << 20
        ),
        name="swiglu",
    )(*[pltpu.with_memory_space_constraint(v, pltpu.HBM) for v in (tokens.T, gate_weight, up_weight, down_weight.T, cotangent.T)])
    mixed, gtok, ggate, gup, gdown = pl.pallas_call(
        place,
        out_shape=outs,
        in_specs=[pl.BlockSpec(memory_space=vm)] * 5,
        out_specs=[pl.BlockSpec(memory_space=vm)] * 5,
        compiler_params=pltpu.CompilerParams(vmem_limit_bytes=8 << 20),
        name="place",
    )(*results)
    return mixed.T, gtok.T, ggate, gup, gdown.T


def solution(mesh):
    return jax.shard_map(
        per_device,
        mesh=mesh,
        in_specs=(
            P(("dp", "fsdp", "tensor"), None),
            P("fsdp", "tensor"),
            P("fsdp", "tensor"),
            P("tensor", "fsdp"),
            P(("dp", "fsdp", "tensor"), None),
        ),
        out_specs=(
            P(("dp", "fsdp", "tensor"), None),
            P(("dp", "fsdp", "tensor"), None),
            P("fsdp", "tensor"),
            P("fsdp", "tensor"),
            P("tensor", "fsdp"),
        ),
        check_vma=False,
    )
```

```python
import jax
import jax.numpy as jnp
from jax import lax
from jax.experimental import pallas as pl
from jax.experimental.pallas import tpu as pltpu
from jax.sharding import PartitionSpec as P

MESH = pl.DeviceIdType.MESH
F32 = jnp.float32
BF16 = jnp.bfloat16

D = 576
ROWS = 128
DY = 144
HID = 192
TILES = 41
CUTS = (0, 7, 14, 21, 27, 34, 41)
GU_CUTS = 4
FIRST = (27, 0, 15)
WIDE = (4, 4, 3)
PLACE = (0, 4, 8)
PARTS = (0, 1, 2)


def start_of(part, x):
    return (4 * x - 2 * (x // 3), 4 * x - x // 3, 3 * x)[part]


def core_start(part, core):
    return (2 * core, 2 * core, core)[part]


def tn(left, right):
    return lax.dot_general(left, right, (((0,), (0,)), ((), ())), preferred_element_type=F32)


def nt(left, right):
    return lax.dot_general(left, right, (((1,), (1,)), ((), ())), preferred_element_type=F32)


def nn(left, right):
    return jnp.dot(left, right, preferred_element_type=F32)


def store_gate_up(ref, value):
    for r in range(9):
        for q in range(3):
            ref[3 * r + q] = value[16 * r : 16 * r + 16, 128 * q : 128 * q + 128]


def store_down(ref, value):
    for r in range(9):
        ref[27 + r] = value[16 * r : 16 * r + 16, 0:128]
    for i in range(4):
        ref[36 + i] = jnp.concatenate(
            [value[32 * i : 32 * i + 16, 128:192], value[32 * i + 16 : 32 * i + 32, 128:192]], axis=1
        )
    ref[40] = jnp.concatenate([value[128:144, 128:192], jnp.zeros((16, 64), value.dtype)], axis=1)


def load_gate_up(tile):
    return jnp.concatenate(
        [jnp.concatenate([tile(3 * r + q) for q in range(3)], axis=1) for r in range(9)], axis=0
    )


def load_down(tile):
    rows = []
    for r in range(9):
        last = tile(36 + r // 2)
        rows.append(jnp.concatenate([tile(27 + r), last[:, 0:64] if r % 2 == 0 else last[:, 64:128]], axis=1))
    return jnp.concatenate(rows, axis=0)


def kernel(
    tok_ref, gate_ref, up_ref, down_ref, cot_ref,
    mixed_ref, gtok_ref, ggate_ref, gup_ref, gdown_ref,
    xs, win, wmine, wrows, wall, swi, slo, ggu, hid, sib_out, own, sib_in, xsend, xrecv, xopp,
    ysend, down_early, xyr, zs, zr, zhsend, zhrecv, fin,
    in_s, tok_s, tok_r, fwd_s, fwd_r, wz_s, wz_r, wy_s, wy_r, opp_s, opp_r,
    sib_s, sib_r, tro_s, tro_r, tr_s, tr_r, xy_s, xy_r, gz_s, gz_r, zh_s, zh_r, ag_s, ag_r,
):
    dp = lax.axis_index("dp")
    y = lax.axis_index("fsdp")
    zl = lax.axis_index("tensor")
    x, zh, c = dp // 4, (dp // 2) % 2, dp % 2
    z = zh * 8 + zl
    sib_c = 1 - c
    home = zl // 4

    def dev(xx, yy, zz, cc):
        zz = (zz + 16) % 16
        return (((xx + 4) % 4) * 4 + (zz // 8) * 2 + cc, (yy + 4) % 4, zz % 8)

    def group(dx, dc):
        return dev(x + dx, y, z, c if dc == 0 else sib_c)

    k_to = (c + home) % 2
    local = jnp.logical_and(x == 0, k_to == 0)
    remote = jnp.logical_not(local)

    def z_to(i):
        return dev(x, y, z + jnp.where(x == 0, 4 - 8 * (i % 2), 4 * k_to - x), home)


    shift = [jnp.where(((zl + r) % 4 + 4 * c - zl + 8) % 8 == r, r - 4, r) for r in range(4)]

    def rcopy(src, dst, ssem, rsem, to):
        return pltpu.make_async_remote_copy(
            src_ref=src, dst_ref=dst, send_sem=ssem, recv_sem=rsem, device_id=to, device_id_type=MESH
        )

    inputs = [
        pltpu.make_async_copy(gate_ref, win.at[0], in_s.at[0]),
        pltpu.make_async_copy(up_ref, win.at[1], in_s.at[0]),
        pltpu.make_async_copy(down_ref, win.at[2], in_s.at[0]),
        pltpu.make_async_copy(tok_ref, xs.at[0, 0], in_s.at[1]),
        pltpu.make_async_copy(cot_ref, xs.at[1, 0], in_s.at[1]),
    ]
    for cp in inputs:
        cp.start()

    def arrived(ref, sem):
        rcopy(ref, ref, sem, sem, group(0, 1)).wait_recv()

    def sent(ref, sem):
        rcopy(ref, ref, sem, sem, group(0, 1)).wait_send()

    barrier = pltpu.get_barrier_semaphore()

    def greet(to):
        pl.semaphore_signal(barrier, inc=1, device_id=to, device_id_type=MESH)

    for dx in (1, 3):
        greet(group(dx, 0))
    for s in (4, -4, 3, -3, 2, -2, 1, -1):
        for h in range(2):
            greet(dev(x, y, z + s, h))
    for dx in (2, 1, 3, 0):
        for d in (2, 1, 3, 0):
            if d or dx == 2:
                greet(dev(x + dx, y + d, z, c))
        greet(group(dx, 1))

    pltpu.make_async_copy(xs.at[0, pl.ds(0, 2)], xs.at[0, pl.ds(0, 2)], in_s.at[1]).wait()
    pl.semaphore_wait(barrier, 35)

    halves = {1: pl.ds(0, D // 2), 3: pl.ds(D // 2, D // 2)}
    for a in (0, 1):
        for late in (0, 1):
            for dx in (1, 3):
                rows = halves[dx if late else 4 - dx]
                rcopy(
                    xs.at[a, 0, rows], xs.at[a, 2 * (4 - dx), rows], tok_s, tok_r.at[a, late], group(dx, 0)
                ).start()

    pltpu.make_async_copy(win, win, in_s.at[0]).wait()
    store_gate_up(wmine, jnp.concatenate([win[0], win[1]], axis=1))
    store_down(wmine, win[2])

    def cut(ref, i):
        return ref.at[pl.ds(CUTS[i], CUTS[i + 1] - CUTS[i])]

    wz = [
        rcopy(cut(wmine, i), cut(wrows.at[0], i), wz_s, wz_r.at[i], z_to(i)) for i in range(len(CUTS) - 1)
    ]

    @pl.when(remote)
    def _():
        for cp in wz:
            cp.start()

    for a in (0, 1):
        rcopy(xs.at[a, 0], xs.at[a, 1], fwd_s, fwd_r.at[a, 0], group(0, 1)).start()

    @pl.when(local)
    def _():
        wrows[0] = wmine[...]

    def pass_on(a, late):
        arrived(xs.at[a, 2], tok_r.at[a, late])
        for dx in (1, 3):
            rows = halves[4 - dx if late else dx]
            if not late:
                rcopy(xs.at[a, 2 * dx, rows], xs.at[a, 4, rows], opp_s, opp_r.at[a], group(4 - dx, 0)).start()
            rcopy(xs.at[a, 2 * dx, rows], xs.at[a, 2 * dx + 1, rows], fwd_s, fwd_r.at[a, 1], group(0, 1)).start()

    def pass_on_opposite(a):
        arrived(xs.at[a, 4], opp_r.at[a])
        rcopy(xs.at[a, 4], xs.at[a, 5], fwd_s, fwd_r.at[a, 2], group(0, 1)).start()

    def wait_pair(a, dx):
        if dx != 3:
            arrived(xs.at[a, pl.ds(2, 2)] if dx == 1 else xs.at[a, 5], fwd_r.at[a, dx])

    for i in range(len(CUTS) - 1):

        @pl.when(remote)
        def _(i=i):
            arrived(cut(wrows.at[0], i), wz_r.at[i])

        for d in (2, 1, 3):
            rcopy(
                cut(wrows.at[0], i), cut(wrows.at[4 - d], i), wy_s, wy_r.at[i], dev(x, y + d, z, c)
            ).start()
        if i in (0, 2, 4, 5):
            pass_on(int(i > 2), int(i in (2, 5)))

    def from_y(i):
        arrived(wrows.at[pl.ds(1, 3), pl.ds(CUTS[i], CUTS[i + 1] - CUTS[i])], wy_r.at[i])

    def pair(a, dx):
        return jnp.concatenate([xs[a, 2 * dx], xs[a, 2 * dx + 1]], axis=1)

    pass_on_opposite(0)
    for i in range(GU_CUTS):
        from_y(i)
    for d in range(4):
        rows = pl.ds(pl.multiple_of(((y + d) % 4) * DY, 16), DY)
        wall[rows, 0 : 2 * HID] = load_gate_up(lambda t: wrows[d, t])
    for dx in (0, 1, 3, 2):
        if dx == 2:
            pass_on_opposite(1)
        cols = pl.ds(dx * 256, 256)
        wait_pair(0, dx)
        sums = tn(wall[:, 0 : 2 * HID], pair(0, dx))
        gate_sum, up_sum = sums[0:HID], sums[HID : 2 * HID]
        sig = 1.0 / (1.0 + jnp.exp(-gate_sum))
        swished = gate_sum * sig
        swi[:, cols] = swished
        slo[:, cols] = up_sum * sig * (1.0 + gate_sum * (1.0 - sig))
        hid[:, cols] = (swished * up_sum).astype(BF16)
    for dx in (0, 1, 3):
        wait_pair(1, dx)
    early = jnp.concatenate([xs[1, n] for n in (0, 1, 2, 3, 6, 7)], axis=1)
    down_early[...] = nt(early, jnp.concatenate([hid[:, 0:512], hid[:, 768:1024]], axis=1))
    wait_pair(1, 2)

    def spread(p, d):
        for dx in (2, 1, 3, 0):
            piece = ysend.at[(y + d) % 4, pl.ds(FIRST[p] + start_of(p, (x + dx) % 4), WIDE[p])]
            there = ((4 - dx) % 4) * 4 + (4 - d) % 4
            place = pl.ds(PLACE[p], WIDE[p])
            if d or dx:
                rcopy(piece, xyr.at[there, place], xy_s, xy_r.at[p], dev(x + dx, y + d, z, c)).start()
            else:
                xyr[0, place] = piece[...]

    down_grad = (down_early[...] + nt(pair(1, 2), hid[:, 512:768])).astype(BF16)
    for n in range(4):
        store_down(ysend.at[n], down_grad[DY * n : DY * n + DY])
    for d in (2, 1, 3, 0):
        spread(0, d)
    for i in range(GU_CUTS, len(CUTS) - 1):
        from_y(i)
    for d in range(4):
        rows = pl.ds(pl.multiple_of(((y + d) % 4) * DY, 16), DY)
        wall[rows, 2 * HID : 3 * HID] = load_down(lambda t: wrows[d, t])
    for dx in (0, 1, 3, 2):
        cols = pl.ds(dx * 256, 256)
        grad_hidden = tn(wall[:, 2 * HID : 3 * HID], pair(1, dx))
        ggu[0:HID, cols] = (grad_hidden * slo[:, cols]).astype(BF16)
        ggu[HID : 2 * HID, cols] = (grad_hidden * swi[:, cols]).astype(BF16)
    gate_up_grad = nt(jnp.concatenate([xs[0, n] for n in range(8)], axis=1), ggu[...]).astype(BF16)
    for n in range(4):
        store_gate_up(ysend.at[n], gate_up_grad[DY * n : DY * n + DY])
    for p in (1, 2):
        for d in (2, 1, 3, 0):
            spread(p, d)

    for dx in (2, 1, 3, 0):
        cols = pl.ds(dx * 256, 256)
        for a in (0, 1):
            part = nn(wall[:, 2 * HID : 3 * HID], hid[:, cols]) if a == 0 else nn(wall[:, 0 : 2 * HID], ggu[:, cols])
            own[a, dx] = part[:, 0:ROWS]
            sib_out[dx, a] = part[:, ROWS : 2 * ROWS].astype(BF16)
            rcopy(
                sib_out.at[dx, a], sib_in.at[dx, a], sib_s, sib_r.at[0 if dx == 2 else 1], group(0, 1)
            ).start()
    arrived(sib_in.at[2], sib_r.at[0])
    for a in (0, 1):
        xsend[a, 2] = (own[a, 2] + sib_in[2, a].astype(F32)).astype(BF16)
        for dx in (1, 3):
            rcopy(xsend.at[a, 2, halves[dx]], xopp.at[a, halves[dx]], tro_s, tro_r, group(dx, 0)).start()

    keep = c != home
    for p in PARTS:
        arrived(xyr.at[pl.ds(1, 15), pl.ds(PLACE[p], WIDE[p])], xy_r.at[p])
        for r in (0, 3, 1, 2):
            there = ((r - x + 4) % 4) * 4
            total = xyr[there, PLACE[p] : PLACE[p] + WIDE[p]].astype(F32)
            for d in (1, 2, 3):
                total = total + xyr[there + d, PLACE[p] : PLACE[p] + WIDE[p]].astype(F32)
            total = total.astype(BF16)
            slot = (shift[r] + 8) % 8
            for h in range(2):
                zs[p, r, h] = total[core_start(p, h) : core_start(p, h) + 2]
                far = jnp.where(shift[r] == -4, 4 - 8 * h, shift[r])
                step = rcopy(zs.at[p, r, h], zr.at[p, slot], gz_s, gz_r.at[p], dev(x, y, z + far, h))
                if r:
                    step.start()
                else:
                    stays = jnp.logical_and(keep, c == h)

                    @pl.when(jnp.logical_not(stays))
                    def _(step=step):
                        step.start()

                    @pl.when(stays)
                    def _(p=p, h=h):
                        zr[p, 0] = zs[p, 0, h]

    arrived(sib_in.at[pl.ds(0, 3)], sib_r.at[1])
    arrived(xopp, tro_r)
    for a in (0, 1):
        for dx in (1, 3):
            part = own[a, dx] + sib_in[dx, a].astype(F32)
            extra = xopp[a, halves[dx]].astype(F32)
            if dx == 1:
                part = jnp.concatenate([part[0 : D // 2] + extra, part[D // 2 : D]], axis=0)
            else:
                part = jnp.concatenate([part[0 : D // 2], part[D // 2 : D] + extra], axis=0)
            xsend[a, dx] = part.astype(BF16)
            rcopy(xsend.at[a, dx], xrecv.at[a, (4 - dx) // 2], tr_s, tr_r.at[a], group(dx, 0)).start()

    for p in PARTS:

        @pl.when(keep)
        def _(p=p):
            arrived(zr.at[p, pl.ds(1, 7)], gz_r.at[p])

        @pl.when(jnp.logical_not(keep))
        def _(p=p):
            arrived(zr.at[p], gz_r.at[p])

        total = zr[p, 0].astype(F32)
        for s in range(1, 8):
            total = total + zr[p, s].astype(F32)
        zhsend[p] = total.astype(BF16)
        for n in range(2):
            rcopy(zhsend.at[p], zhrecv.at[p, n], zh_s, zh_r.at[p], dev(x, y, z + 4 - 8 * n, c)).start()

    me = x * 2 + c
    for p in PARTS:
        arrived(zhrecv.at[p], zh_r.at[p])
        fin[me, p] = (zhrecv[p, 0].astype(F32) + zhrecv[p, 1].astype(F32)).astype(BF16)
        for dx in (2, 1, 3, 0):
            for dc in (1, 0):
                if dx or dc:
                    rcopy(fin.at[me, p], fin.at[me, p], ag_s, ag_r.at[p], group(dx, dc)).start()
    for a, out in ((0, mixed_ref), (1, gtok_ref)):
        arrived(xrecv.at[a], tr_r.at[a])
        total = own[a, 0] + sib_in[0, a].astype(F32)
        for n in range(2):
            total = total + xrecv[a, n].astype(F32)
        out[...] = total.astype(BF16)

    for p in PARTS:
        arrived(fin.at[pl.ds(0, 7), p], ag_r.at[p])

    def summed(t):
        p = 0 if t >= FIRST[0] else 1 if t < FIRST[2] else 2
        over = [n for n in range(4) if 0 <= t - FIRST[p] - start_of(p, n) < WIDE[p]][0]
        u = t - FIRST[p] - start_of(p, over)
        half = 0 if u < 2 else 1
        return fin[2 * over + half, p, u - core_start(p, half)]

    whole = load_gate_up(summed)
    ggate_ref[...] = whole[:, 0:HID]
    gup_ref[...] = whole[:, HID : 2 * HID]
    gdown_ref[...] = load_down(summed)

    @pl.when(remote)
    def _():
        sent(wmine, wz_s)

    @pl.when(keep)
    def _():
        sent(zr.at[pl.ds(0, 3), pl.ds(1, 7)], gz_s)

    @pl.when(jnp.logical_not(keep))
    def _():
        sent(zr, gz_s)

    sent(xs.at[0, pl.ds(0, 4)], tok_s)
    sent(xs.at[0, pl.ds(0, 2)], opp_s)
    sent(xs.at[0], fwd_s)
    sent(wrows.at[pl.ds(1, 3)], wy_s)
    sent(xyr.at[pl.ds(1, 15)], xy_s)
    sent(sib_out, sib_s)
    sent(xopp, tro_s)
    sent(xrecv, tr_s)
    sent(zhrecv, zh_s)
    sent(fin.at[pl.ds(0, 7)], ag_s)


def place(*refs):
    for i, o in zip(refs[:5], refs[5:]):
        o[...] = i[...]


def per_device(tokens, gate_weight, up_weight, down_weight, cotangent):
    dma = pltpu.SemaphoreType.DMA
    vm = pltpu.VMEM
    outs = (
        jax.ShapeDtypeStruct((D, ROWS), BF16),
        jax.ShapeDtypeStruct((D, ROWS), BF16),
        jax.ShapeDtypeStruct((DY, HID), BF16),
        jax.ShapeDtypeStruct((DY, HID), BF16),
        jax.ShapeDtypeStruct((DY, HID), BF16),
    )
    pieces = len(CUTS) - 1
    results = pl.pallas_call(
        kernel,
        out_shape=outs,
        in_specs=[pl.BlockSpec(memory_space=pl.ANY)] * 5,
        out_specs=[pl.BlockSpec(memory_space=vm)] * 5,
        scratch_shapes=[
            vm((2, 8, D, ROWS), BF16),
            vm((3, DY, HID), BF16),
            vm((TILES, 16, 128), BF16),
            vm((4, TILES, 16, 128), BF16),
            vm((D, 3 * HID), BF16),
            vm((HID, 8 * ROWS), F32),
            vm((HID, 8 * ROWS), F32),
            vm((2 * HID, 8 * ROWS), BF16),
            vm((HID, 8 * ROWS), BF16),
            vm((4, 2, D, ROWS), BF16),
            vm((2, 4, D, ROWS), F32),
            vm((4, 2, D, ROWS), BF16),
            vm((2, 4, D, ROWS), BF16),
            vm((2, 2, D, ROWS), BF16),
            vm((2, D, ROWS), BF16),
            vm((4, TILES, 16, 128), BF16),
            vm((D, HID), F32),
            vm((16, sum(WIDE), 16, 128), BF16),
            vm((3, 4, 2, 2, 16, 128), BF16),
            vm((3, 8, 2, 16, 128), BF16),
            vm((3, 2, 16, 128), BF16),
            vm((3, 2, 2, 16, 128), BF16),
            vm((8, 3, 2, 16, 128), BF16),
            dma((2,)),
            dma, dma((2, 2)),
            dma, dma((2, 3)),
            dma, dma((pieces,)),
            dma, dma((pieces,)),
            dma, dma((2,)),
            dma, dma((2,)),
            dma, dma,
            dma, dma((2,)),
            dma, dma((3,)),
            dma, dma((3,)),
            dma, dma((3,)),
            dma, dma((3,)),
        ],
        compiler_params=pltpu.CompilerParams(
            collective_id=0, has_side_effects=True, vmem_limit_bytes=40 << 20
        ),
        name="swiglu",
    )(*[pltpu.with_memory_space_constraint(v, pltpu.HBM) for v in (tokens.T, gate_weight, up_weight, down_weight.T, cotangent.T)])
    mixed, gtok, ggate, gup, gdown = pl.pallas_call(
        place,
        out_shape=outs,
        in_specs=[pl.BlockSpec(memory_space=vm)] * 5,
        out_specs=[pl.BlockSpec(memory_space=vm)] * 5,
        compiler_params=pltpu.CompilerParams(vmem_limit_bytes=8 << 20),
        name="place",
    )(*results)
    return mixed.T, gtok.T, ggate, gup, gdown.T


def solution(mesh):
    return jax.shard_map(
        per_device,
        mesh=mesh,
        in_specs=(
            P(("dp", "fsdp", "tensor"), None),
            P("fsdp", "tensor"),
            P("fsdp", "tensor"),
            P("tensor", "fsdp"),
            P(("dp", "fsdp", "tensor"), None),
        ),
        out_specs=(
            P(("dp", "fsdp", "tensor"), None),
            P(("dp", "fsdp", "tensor"), None),
            P("fsdp", "tensor"),
            P("fsdp", "tensor"),
            P("tensor", "fsdp"),
        ),
        check_vma=False,
    )
```
